256 devices in a mesh: seq: 32 (over z, x), clip: 8 (over y, core).
Axes of the slice: x: 4, y: 4, z: 8, core: 2. Of those that a mesh axis runs over, the one named last changes fastest.
Arguments:
- tokens: bfloat16 [8, 16384, 1280], P('clip', 'seq'), may hold values from -24 to 24
- slot_weight: bfloat16 [1280, 256], replicated, may hold values from -2 to 2
- pattern: int32 [128, 16], P('seq'), may hold values from 0 to 63, all different within a row
- w_in: bfloat16 [64, 1280, 5120], P('seq', None, 'clip'), may hold values from -0.15625 to 0.15625
- w_out: bfloat16 [64, 5120, 1280], P('seq', 'clip'), may hold values from -0.078125 to 0.078125
Outputs:
- mixed: bfloat16 [8, 16384, 1280], P('clip', 'seq')
The draws below stay inside these ranges and needn't reach their ends.
Inputs may be any that keep to these rules, and one draw needn't show every extreme that they name: `pattern`: each row names 16 different groups, and every group is named by some row.
All inputs are finite; a program needn't handle non-finite values.
Results may differ from the reference program's by a relative error of at most 0.0095.
Values may be sent and summed in bfloat16 or wider, within the bound.
A program may use at most 128 MiB of HBM per device.

```python
import math
import jax
import jax.numpy as jnp
from jax import lax

D = 1280
FF = 5120
SLOTS = 4
BLOCK = 128
EXPERTS = 64
SLOTS_ALL = 256
SEQLEN = 16384
CLIPS = 8
NBLK = 128
TOPG = 16


def slot_columns(key):
    base = jax.random.truncated_normal(jax.random.fold_in(key, 11), -4.0, 4.0, (D, SLOTS_ALL), jnp.float32)
    return base * (3.0 / math.sqrt(D))


def draw_slot_weight(key, part):
    columns = slot_columns(key)
    return columns.astype(jnp.bfloat16)


def draw_tokens(key, part):
    key = jax.random.fold_in(key, 3)
    key_base = jax.random.fold_in(key, 0)
    base = jax.random.truncated_normal(key_base, -6.0, 6.0, (CLIPS, SEQLEN, D), jnp.float32)
    return base.astype(jnp.bfloat16)


def shard_levels(rng, dims, pieces, smallest, largest):
    level, own = 1.0, jax.random.fold_in(rng, 6)
    for axis_at, shards_of in pieces:
        draws = jnp.exp(jax.random.uniform(jax.random.fold_in(own, axis_at), (shards_of,), jnp.float32, smallest / len(pieces), largest / len(pieces)))
        level = level * jnp.repeat(draws, dims[axis_at] // shards_of).reshape([-1 if axis == axis_at else 1 for axis in range(len(dims))])
    return level


def picks_of(own_key, rows, count, top, lift):
    ranking = jax.random.permutation(jax.random.fold_in(own_key, 1), count)
    favour = ranking
    for power in range(3):
        favour = favour * favour // count
    favour = favour * lift // count
    chance = jax.random.randint(jax.random.fold_in(own_key, 2), (rows, count), 0, 4096) + favour
    holders = jax.random.permutation(jax.random.fold_in(own_key, 3), rows)[jnp.arange(count) % rows]
    chance = jnp.where(jnp.arange(rows)[:, None] == holders[None, :], 1 << 14, chance)
    priority = chance * count + jnp.arange(count)
    return lax.top_k(priority.astype(jnp.int32), top)[1].astype(jnp.int32)


def gaussian(own_key, dims, spread, bound, pieces=(), kind=jnp.bfloat16):
    values = jax.random.normal(own_key, dims, jnp.float32) * spread
    if len(pieces) > 0:
        values = shard_levels(own_key, dims, pieces, -0.22, 0.18) * values
    return jnp.clip(values, min=-bound, max=bound).astype(kind)


def setup_inputs(seed: int = 0) -> dict:
    keys = jax.random.split(jax.random.key(seed), 6)
    return {
        "tokens": draw_tokens(jax.random.fold_in(keys[5], 71), 0),
        "slot_weight": draw_slot_weight(jax.random.fold_in(keys[5], 71), 0),
        "pattern": picks_of(keys[2], NBLK, EXPERTS, TOPG, 0),
        "w_in": gaussian(keys[3], (EXPERTS, D, FF), D ** -0.5, 0.15625, ((0, 32), (2, 8))),
        "w_out": gaussian(keys[4], (EXPERTS, FF, D), FF ** -0.5, 0.078125, ((0, 32), (1, 8))),
    }


very_low = -1.0e30


def slot_mask(pattern):
    groups = jnp.arange(SLOTS_ALL, dtype=jnp.int32) // SLOTS
    return jnp.any(pattern[:, :, None] == groups[None, None, :], axis=1)


def dispatch_clip(clip_tokens, slot_weight, allowed):
    logits = jnp.dot(clip_tokens, slot_weight, preferred_element_type=jnp.float32)
    tiled = logits.reshape(NBLK, BLOCK, SLOTS_ALL)
    block_top = jnp.max(tiled, axis=1)
    weights = jnp.exp(tiled - block_top[:, None, :]) * allowed[:, None, :].astype(jnp.float32)
    masses = jnp.sum(weights, axis=1)
    peak = jnp.where(allowed, block_top, very_low)
    top = jnp.max(peak, axis=0)
    factor = jnp.exp(peak - top[None, :])
    rounded = lax.optimization_barrier(weights.astype(jnp.bfloat16)).astype(jnp.float32)
    scaled = (rounded * factor[:, None, :]).reshape(SEQLEN, SLOTS_ALL)
    weighted = jnp.dot(scaled.T, clip_tokens.astype(jnp.float32), precision=lax.Precision.HIGHEST)
    mass = jnp.sum(factor * masses, axis=0)
    return (weighted / mass[:, None]).astype(jnp.bfloat16)


def run_expert(items):
    rows, first, second = items
    flat = rows.reshape(CLIPS * SLOTS, D)
    inner = jnp.dot(flat, first, preferred_element_type=jnp.float32)
    active = jax.nn.gelu(inner, approximate=True).astype(jnp.bfloat16)
    result = jnp.dot(active, second, preferred_element_type=jnp.float32).astype(jnp.bfloat16)
    return result.reshape(CLIPS, SLOTS, D)


def combine_clip(items, slot_weight):
    clip_tokens, clip_outputs = items
    logits = jnp.dot(clip_tokens, slot_weight, preferred_element_type=jnp.float32)
    probs = jax.nn.softmax(logits, axis=-1).astype(jnp.bfloat16)
    return jnp.dot(probs, clip_outputs, preferred_element_type=jnp.float32).astype(jnp.bfloat16)


def reference(tokens, slot_weight, pattern, w_in, w_out):
    allowed = slot_mask(pattern)
    slot_in = lax.map(lambda clip_tokens: dispatch_clip(clip_tokens, slot_weight, allowed), tokens)
    grouped = jnp.transpose(slot_in.reshape(CLIPS, EXPERTS, SLOTS, D), (1, 0, 2, 3))
    produced = lax.map(run_expert, (grouped, w_in, w_out))
    slot_out = jnp.transpose(produced, (1, 0, 2, 3)).reshape(CLIPS, SLOTS_ALL, D)
    return lax.map(lambda items: combine_clip(items, slot_weight), (tokens, slot_out))
```

```python
import functools

import jax
import jax.numpy as jnp
from jax import lax
from jax.experimental import pallas as pl
from jax.experimental.pallas import tpu as pltpu
from jax.sharding import PartitionSpec as P

MESH = pl.DeviceIdType.MESH
BF16, F32 = jnp.bfloat16, jnp.float32
D = 1280
FS = 640
TOK = 512
SLOTS_ALL = 256
ZN, XN, YN = 8, 4, 4
CLIPS = 8
EXT = 128
CHUNKS = (512, 512, 256)
STARTS = tuple(sum(CHUNKS[:i]) for i in range(len(CHUNKS)))
NC = len(CHUNKS)
LOW = -1.0e30
EMPTY = -1.0e29

XP = (2, 1, 3)
ZP = (4, 3, 5, 2, 6, 1, 7)
CP = tuple(range(1, 8))


def pieces(v):
    hi = v.astype(BF16).astype(F32)
    mid = (v - hi).astype(BF16).astype(F32)
    lo = ((v - hi) - mid).astype(BF16).astype(F32)
    return hi, mid, lo


def ext_of(top, mass):
    lane = lax.broadcasted_iota(jnp.int32, (top.shape[0], EXT), 1)
    out = jnp.zeros((top.shape[0], EXT), F32)
    for i, piece in enumerate(pieces(top) + pieces(mass)):
        out = jnp.where(lane == i, piece, out)
    return out


def of_ext(ext):
    e = ext.astype(F32)
    return e[:, 0:1] + e[:, 1:2] + e[:, 2:3], e[:, 3:4] + e[:, 4:5] + e[:, 5:6]


def merge(stats):
    top = stats[0][0]
    for t, _ in stats[1:]:
        top = jnp.maximum(top, t)
    factors = [jnp.exp(t - top) for t, _ in stats]
    mass = factors[0] * stats[0][1]
    for f, (_, m) in zip(factors[1:], stats[1:]):
        mass = mass + f * m
    return factors, top, mass


def pack(v):
    h = v.shape[-1] // 2
    return jnp.concatenate([v[:, :, :h], v[:, :, h:]], axis=1)


def unpack(v):
    n, _, h = v.shape
    f = v.astype(F32)
    return jnp.concatenate([f[:, :8].reshape(n * 8, h), f[:, 8:].reshape(n * 8, h)], axis=1)


def kernel(tok_hbm, sw_hbm, pat_ref, win_hbm, wout_hbm, out_hbm, *scratch):
    it = iter(scratch)
    tok, sw, win, wout = next(it), next(it), next(it), next(it)
    wt_ref, probs, outv = next(it), next(it), next(it)
    psend = [next(it) for _ in range(NC)]
    xbuf = [next(it) for _ in range(NC)]
    zsend = [next(it) for _ in range(NC)]
    zbuf = [next(it) for _ in range(NC)]
    ybuf = [next(it) for _ in range(NC)]
    rsend = [next(it) for _ in range(NC)]
    rbuf = [next(it) for _ in range(NC)]
    agx = [next(it) for _ in range(NC)]
    load_sem, out_sem, send_sem, recv_sem = next(it), next(it), next(it), next(it)

    seq, clip = lax.axis_index("seq"), lax.axis_index("clip")
    z, x = seq // XN, seq % XN
    y, core = clip // 2, clip % 2

    def x_peer(d):
        return {"seq": z * XN + (x + d) % XN, "clip": clip}

    def z_peer(d):
        return {"seq": ((z + d) % ZN) * XN + x, "clip": clip}

    def c_peer(j):
        return {"seq": seq, "clip": ((y + j // 2) % YN) * 2 + (core + j % 2) % 2}

    def c_back(j):
        return {"seq": seq, "clip": ((y + YN - j // 2) % YN) * 2 + (core + j % 2) % 2}

    loads = [
        pltpu.make_async_copy(sw_hbm, sw, load_sem.at[0]),
        pltpu.make_async_copy(tok_hbm, tok, load_sem.at[1]),
        pltpu.make_async_copy(win_hbm, win, load_sem.at[2]),
        pltpu.make_async_copy(wout_hbm, wout, load_sem.at[3]),
    ]
    for load in loads:
        load.start()

    barrier = pltpu.get_barrier_semaphore()
    for peers, peer in ((XP, x_peer), (ZP, z_peer), (CP, c_peer)):
        for d in peers:
            pl.semaphore_signal(barrier, inc=1, device_id=peer(d), device_id_type=MESH)

    def send(stage, c, src, dst, to):
        pltpu.make_async_remote_copy(
            src_ref=src, dst_ref=dst, send_sem=send_sem.at[stage, c],
            recv_sem=recv_sem.at[stage, c], device_id=to, device_id_type=MESH,
        ).start()

    def moved(stage, c, view):
        return pltpu.make_async_remote_copy(
            src_ref=view, dst_ref=view, send_sem=send_sem.at[stage, c],
            recv_sem=recv_sem.at[stage, c], device_id=x_peer(1), device_id_type=MESH,
        )

    views = {}
    for c in range(NC):
        views[0, c] = xbuf[c]
        views[1, c] = zbuf[c]
        views[2, c] = ybuf[c].at[pl.ds(1, 7)]
        views[3, c] = rbuf[c]
        views[4, c] = agx[c].at[0, pl.ds(0, 7)]
        views[5, c] = agx[c].at[pl.ds(0, 3)]

    def arrived(stage, c):
        moved(stage, c, views[stage, c]).wait_recv()

    loads[0].wait()
    loads[1].wait()
    logits = jnp.dot(tok[...], sw[...], preferred_element_type=F32)
    group = lax.broadcasted_iota(jnp.int32, (1, SLOTS_ALL), 1) // 4
    masked = []
    for b in range(4):
        named = group == pat_ref[b, 0]
        for j in range(1, 16):
            named = jnp.logical_or(named, group == pat_ref[b, j])
        masked.append(jnp.where(named, logits[b * 128:(b + 1) * 128], LOW))
    turned = jnp.concatenate(masked, axis=0).T
    turned = jnp.concatenate(
        [turned[(zz * XN + xx) * 8:(zz * XN + xx) * 8 + 8] for xx in range(XN) for zz in range(ZN)],
        axis=0,
    )
    top = jnp.maximum(jnp.max(turned, axis=1, keepdims=True), EMPTY)
    weights = jnp.exp(turned - top)
    mass = jnp.sum(weights, axis=1, keepdims=True)
    wt_ref[...] = weights.astype(BF16)
    psend[0][:, CHUNKS[0]:] = ext_of(top, mass).astype(BF16)
    for c in range(NC):
        s, w = STARTS[c], CHUNKS[c]
        part = jnp.dot(wt_ref[...], tok[:, s:s + w], preferred_element_type=F32)
        psend[c][:, 0:w] = part.astype(BF16)
        if c == 0:
            pl.semaphore_wait(barrier, len(XP) + len(ZP) + len(CP))
        for d in XP:
            rows = pl.ds(pl.multiple_of(((x + d) % XN) * 64, 64), 64)
            send(0, c, psend[c].at[rows], xbuf[c].at[d - 1], x_peer(d))

    e = jnp.exp(logits - jnp.max(logits, axis=1, keepdims=True))
    probs[...] = (e / jnp.sum(e, axis=1, keepdims=True)).astype(BF16)

    state = {}

    def stage_x(c):
        w = CHUNKS[c]
        h = w // 2
        arrived(0, c)
        mine = pl.ds(pl.multiple_of(x * 64, 64), 64)
        if c == 0:
            exts = [psend[0][mine, w:]] + [xbuf[0][k, :, w:] for k in range(3)]
            state["x"] = merge([of_ext(e) for e in exts])
        factors, top, mass = state["x"]
        total = factors[0] * psend[c][mine, 0:w].astype(F32)
        for k in range(3):
            total = total + factors[k + 1] * xbuf[c][k, :, 0:w].astype(F32)
        zsend[c][:, :, 0:h] = pack(total.reshape(ZN, 8, w)).astype(BF16)
        if c == 0:
            e = ext_of(top, mass).reshape(ZN, 8, EXT)
            zsend[c][:, :, h:] = jnp.concatenate([e, e], axis=1).astype(BF16)
        for d in ZP:
            send(1, c, zsend[c].at[(z + d) % ZN], zbuf[c].at[d - 1], z_peer(d))

    def stage_z(c):
        h = CHUNKS[c] // 2
        arrived(1, c)
        if c == 0:
            exts = [zsend[0][z, :, h:]] + [zbuf[0][k, :, h:] for k in range(7)]
            factors, _, mass = merge([of_ext(e) for e in exts])
            state["z"] = [f / mass for f in factors]
        factors = state["z"]
        total = factors[0] * zsend[c][z, :, 0:h].astype(F32)
        for k in range(7):
            total = total + factors[k + 1] * zbuf[c][k, :, 0:h].astype(F32)
        ybuf[c][0] = total.astype(BF16)
        for j in CP:
            send(2, c, ybuf[c].at[0], ybuf[c].at[j], c_peer(j))

    def stage_in(c):
        s, w = STARTS[c], CHUNKS[c]
        arrived(2, c)
        if c == 0:
            loads[2].wait()
        rows = unpack(ybuf[c][...]).astype(BF16)
        inner = [jnp.dot(rows, win[e, s:s + w, :], preferred_element_type=F32) for e in range(2)]
        if c == 0:
            state["inner"] = inner
        else:
            state["inner"] = [a + b for a, b in zip(state["inner"], inner)]

    def stage_out(c):
        s, w = STARTS[c], CHUNKS[c]
        if c == 0:
            loads[3].wait()
            first = lax.broadcasted_iota(jnp.int32, (64, FS), 0) % 8 < 4
            act = jax.nn.gelu(jnp.where(first, *state["inner"]), approximate=True)
            state["active"] = [
                jnp.where(first, act, 0.0).astype(BF16), jnp.where(first, 0.0, act).astype(BF16)]
        outer = jnp.dot(state["active"][0], wout[0, :, s:s + w], preferred_element_type=F32)
        outer = outer + jnp.dot(state["active"][1], wout[1, :, s:s + w], preferred_element_type=F32)
        rsend[c][...] = pack(outer.reshape(CLIPS, 8, w)).astype(BF16)
        for j in CP:
            send(3, c, rsend[c].at[j], rbuf[c].at[j - 1], c_back(j))

    def stage_sum(c):
        arrived(3, c)
        total = rsend[c][0].astype(F32)
        for k in range(7):
            total = total + rbuf[c][k].astype(F32)
        agx[c][x, z] = total.astype(BF16)
        for d in ZP:
            send(4, c, agx[c].at[x, z], agx[c].at[x, z], z_peer(d))

    def stage_spread(c):
        arrived(4, c)
        for d in XP:
            send(5, c, agx[c].at[x], agx[c].at[x], x_peer(d))

    def stage_mix(c):
        s, w = STARTS[c], CHUNKS[c]
        arrived(5, c)
        rows = [agx[c][xx].astype(F32) for xx in range(XN)]
        table = jnp.concatenate(
            [jnp.concatenate([rows[xx][zz, :8], rows[xx][zz, 8:]], axis=1)
             for zz in range(ZN) for xx in range(XN)],
            axis=0,
        ).astype(BF16)
        mixed = jnp.dot(probs[...], table, preferred_element_type=F32)
        outv[:, s:s + w] = mixed.astype(BF16)
        pltpu.make_async_copy(
            outv.at[:, pl.ds(s, w)], out_hbm.at[:, pl.ds(s, w)], out_sem.at[c]).start()

    def pipeline(stages):
        n = len(stages)
        for step in range(NC + n - 1):
            for i in range(n):
                if 0 <= step - i < NC:
                    stages[i](step - i)

    pipeline([stage_x, stage_z, stage_in])
    pipeline([stage_out, stage_sum, stage_spread, stage_mix])

    for stage in range(6):
        for c in range(NC):
            moved(stage, c, views[stage, c]).wait_send()
    for c in range(NC):
        s, w = STARTS[c], CHUNKS[c]
        pltpu.make_async_copy(
            outv.at[:, pl.ds(s, w)], out_hbm.at[:, pl.ds(s, w)], out_sem.at[c]).wait()


def local(tokens, slot_weight, pattern, w_in, w_out):
    def vm(*shape):
        return pltpu.VMEM(shape, BF16)

    halves = [w // 2 for w in CHUNKS]
    ext = [EXT if c == 0 else 0 for c in range(NC)]
    scratch = [vm(TOK, D), vm(D, SLOTS_ALL), vm(2, D, FS), vm(2, FS, D)]
    scratch += [vm(SLOTS_ALL, TOK), vm(TOK, SLOTS_ALL), vm(TOK, D)]
    scratch += [vm(SLOTS_ALL, CHUNKS[c] + ext[c]) for c in range(NC)]
    scratch += [vm(3, 64, CHUNKS[c] + ext[c]) for c in range(NC)]
    scratch += [vm(ZN, 16, halves[c] + ext[c]) for c in range(NC)]
    scratch += [vm(7, 16, halves[c] + ext[c]) for c in range(NC)]
    scratch += [vm(CLIPS, 16, halves[c]) for c in range(NC)]
    scratch += [vm(CLIPS, 16, halves[c]) for c in range(NC)]
    scratch += [vm(7, 16, halves[c]) for c in range(NC)]
    scratch += [vm(XN, ZN, 16, halves[c]) for c in range(NC)]
    scratch += [
        pltpu.SemaphoreType.DMA((4,)), pltpu.SemaphoreType.DMA((NC,)),
        pltpu.SemaphoreType.DMA((6, NC)), pltpu.SemaphoreType.DMA((6, NC)),
    ]
    hbm = pl.BlockSpec(memory_space=pl.ANY)
    out = pl.pallas_call(
        kernel,
        out_shape=jax.ShapeDtypeStruct((TOK, D), BF16),
        in_specs=[hbm, hbm, pl.BlockSpec(memory_space=pltpu.SMEM), hbm, hbm],
        out_specs=hbm,
        scratch_shapes=scratch,
        compiler_params=pltpu.CompilerParams(
            collective_id=0, has_side_effects=True, vmem_limit_bytes=56 << 20),
        name="layer",
    )(tokens.reshape(TOK, D), slot_weight, pattern, w_in, w_out)
    return out.reshape(tokens.shape)


def solution(mesh):
    in_specs = (
        P("clip", "seq", None),
        P(),
        P("seq", None),
        P("seq", None, "clip"),
        P("seq", "clip", None),
    )
    return jax.shard_map(
        local, mesh=mesh, in_specs=in_specs, out_specs=P("clip", "seq", None), check_vma=False)
```

```python
import jax
import jax.numpy as jnp
from jax import lax
from jax.experimental import pallas as pl
from jax.experimental.pallas import tpu as pltpu
from jax.sharding import PartitionSpec as P

MESH = pl.DeviceIdType.MESH
BF16, F32 = jnp.bfloat16, jnp.float32
D = 1280
FS = 640
TOK = 512
SLOTS_ALL = 256
ZN, XN, YN = 8, 4, 4
EXT = 128
CHUNKS = (512, 512, 256)
STARTS = tuple(sum(CHUNKS[:i]) for i in range(len(CHUNKS)))
NC = len(CHUNKS)
ORDER_IN = ((0, 0), (0, 1), (0, 2), (1, 0), (1, 1), (1, 2))
ORDER_OUT = ((0, 0), (0, 1), (0, 2), (1, 0), (1, 1), (1, 2))
PART = 256
LOW = -1.0e30
EMPTY = -1.0e29

XP = (2, 1, 3)
ZP = (4, 3, 5, 2, 6, 1, 7)
YP = (2, 1, 3)


def pieces(v):
    hi = v.astype(BF16).astype(F32)
    mid = (v - hi).astype(BF16).astype(F32)
    lo = ((v - hi) - mid).astype(BF16).astype(F32)
    return hi, mid, lo


def ext_of(top, mass):
    lane = lax.broadcasted_iota(jnp.int32, (top.shape[0], EXT), 1)
    out = jnp.zeros((top.shape[0], EXT), F32)
    for i, piece in enumerate(pieces(top) + pieces(mass)):
        out = jnp.where(lane == i, piece, out)
    return out


def of_ext(ext):
    e = ext.astype(F32)
    return e[:, 0:1] + e[:, 1:2] + e[:, 2:3], e[:, 3:4] + e[:, 4:5] + e[:, 5:6]


def merge(stats):
    top = stats[0][0]
    for t, _ in stats[1:]:
        top = jnp.maximum(top, t)
    factors = [jnp.exp(t - top) for t, _ in stats]
    mass = factors[0] * stats[0][1]
    for f, (_, m) in zip(factors[1:], stats[1:]):
        mass = mass + f * m
    return factors, top, mass


def pack(v):
    h = v.shape[-1] // 2
    return jnp.concatenate([v[:, :, :h], v[:, :, h:]], axis=1)


def kernel(tok_hbm, sw_hbm, pat_hbm, win_hbm, wout_hbm, probs, table_ref, *scratch):
    it = iter(scratch)
    tok, sw, pat, win, wout, wt_ref = (next(it) for _ in range(6))
    psend, xbuf, zsend, zbuf, ybuf, rsend, rbuf, agx = (
        [next(it) for _ in range(NC)] for _ in range(8))
    load_sem, send_sem, recv_sem = next(it), next(it), next(it)

    seq, clip = lax.axis_index("seq"), lax.axis_index("clip")
    z, x = seq // XN, seq % XN
    y, core = clip // 2, clip % 2

    def dev(dz, dx, dy, k):
        return {
            "seq": ((z + dz) % ZN) * XN + (x + dx) % XN, "clip": ((y + dy) % YN) * 2 + k}

    pat_load = pltpu.make_async_copy(pat_hbm, pat, load_sem.at[0])
    sw_load = pltpu.make_async_copy(sw_hbm, sw, load_sem.at[1])
    tok_loads = [
        pltpu.make_async_copy(
            tok_hbm.at[pl.ds(i * PART, PART)], tok.at[pl.ds(i * PART, PART)], load_sem.at[2 + i])
        for i in range(TOK // PART)
    ]
    win_load = pltpu.make_async_copy(win_hbm, win, load_sem.at[6])
    wout_load = pltpu.make_async_copy(wout_hbm, wout, load_sem.at[7])
    sw_load.start()
    for load in tok_loads:
        load.start()
    pat_load.start()

    barrier = pltpu.get_barrier_semaphore()

    def greet(*to):
        pl.semaphore_signal(barrier, inc=1, device_id=dev(*to), device_id_type=MESH)

    for d in XP:
        greet(0, d, 0, 1)
    for d in YP:
        greet(0, 0, d, 1)

    @pl.when(core == 0)
    def _():
        greet(0, 0, 0, 1)

    @pl.when(core == 1)
    def _():
        greet(0, 0, 0, 0)
        for d in XP:
            greet(0, d, 0, 0)
        for d in YP:
            greet(0, 0, d, 0)
        for d in ZP:
            greet(d, 0, 0, 1)

    def send(stage, c, src, dst, to, sent=None):
        pltpu.make_async_remote_copy(
            src_ref=src, dst_ref=dst, send_sem=send_sem.at[stage if sent is None else sent, c],
            recv_sem=recv_sem.at[stage, c], device_id=dev(*to), device_id_type=MESH,
        ).start()

    def moved(stage, c, view):
        return pltpu.make_async_remote_copy(
            src_ref=view, dst_ref=view, send_sem=send_sem.at[stage, c],
            recv_sem=recv_sem.at[min(stage, 5), c], device_id=dev(0, 1, 0, 1), device_id_type=MESH,
        )

    sw_load.wait()
    logits = []
    for i in range(TOK // PART):
        tok_loads[i].wait()
        logits.append(
            jnp.dot(tok[i * PART:(i + 1) * PART], sw[...], preferred_element_type=F32))
    logits = jnp.concatenate(logits, axis=0)
    win_load.start()
    wout_load.start()
    pat_load.wait()
    group = lax.broadcasted_iota(jnp.int32, (1, SLOTS_ALL), 1) // 4
    masked = []
    for b in range(4):
        named = group == pat[b, 0]
        for j in range(1, 16):
            named = jnp.logical_or(named, group == pat[b, j])
        masked.append(jnp.where(named, logits[b * 128:(b + 1) * 128], LOW))
    turned = jnp.concatenate(masked, axis=0).T
    turned = jnp.concatenate(
        [turned[(zz * XN + xx) * 8:(zz * XN + xx) * 8 + 8] for xx in range(XN) for zz in range(ZN)],
        axis=0,
    )
    top = jnp.maximum(jnp.max(turned, axis=1, keepdims=True), EMPTY)
    weights = jnp.exp(turned - top)
    mass = jnp.sum(weights, axis=1, keepdims=True)
    wt_ref[...] = weights.astype(BF16)
    psend[0][:, CHUNKS[0]:] = ext_of(top, mass).astype(BF16)
    for c in range(NC):
        s, w = STARTS[c], CHUNKS[c]
        part = jnp.dot(wt_ref[...], tok[:, s:s + w], preferred_element_type=F32)
        psend[c][:, 0:w] = part.astype(BF16)

        @pl.when(core == 0)
        def _():
            if c == 0:
                pl.semaphore_wait(barrier, 7)
            for d in XP + (0,):
                rows = pl.ds(pl.multiple_of(((x + d) % XN) * 64, 64), 64)
                send(0, c, psend[c].at[rows], xbuf[c].at[3 + d], (0, d, 0, 1))

        @pl.when(core == 1)
        def _():
            if c == 0:
                pl.semaphore_wait(barrier, 20)
            for d in XP:
                rows = pl.ds(pl.multiple_of(((x + d) % XN) * 64, 64), 64)
                send(0, c, psend[c].at[rows], xbuf[c].at[d - 1], (0, d, 0, 1))

    e = jnp.exp(logits - jnp.max(logits, axis=1, keepdims=True))
    probs[...] = (e / jnp.sum(e, axis=1, keepdims=True)).astype(BF16)

    state = {}

    def stage_x(c):
        w = CHUNKS[c]
        mine = pl.ds(pl.multiple_of(x * 64, 64), 64)
        moved(0, c, xbuf[c]).wait_recv()

        def sources(lanes):
            return (
                [xbuf[c][k, :, lanes] for k in range(3, 7)],
                [psend[c][mine, lanes]] + [xbuf[c][k, :, lanes] for k in range(3)],
            )

        if c == 0:
            state["x"] = [merge([of_ext(e) for e in exts]) for exts in sources(slice(w, w + EXT))]
            exts = [ext_of(t, m).reshape(ZN, 8, EXT) for _, t, m in state["x"]]
            zsend[0][:, :, w:] = jnp.concatenate(exts, axis=1).astype(BF16)
        totals = []
        for (factors, _, _), parts in zip(state["x"], sources(slice(0, w))):
            total = factors[0] * parts[0].astype(F32)
            for f, p in zip(factors[1:], parts[1:]):
                total = total + f * p.astype(F32)
            totals.append(total.reshape(ZN, 8, w))
        zsend[c][:, :, 0:w] = jnp.concatenate(totals, axis=1).astype(BF16)
        for d in ZP:
            send(1, c, zsend[c].at[(z + d) % ZN], zbuf[c].at[d - 1], (d, 0, 0, 1))

    def stage_z(c):
        w = CHUNKS[c]
        moved(1, c, zbuf[c]).wait_recv()
        if c == 0:
            exts = [zsend[0][z, :, w:]] + [zbuf[0][k, :, w:] for k in range(7)]
            factors, _, mass = merge([of_ext(e) for e in exts])
            state["z"] = [f / mass for f in factors]
        factors = state["z"]
        total = factors[0] * zsend[c][z, :, 0:w].astype(F32)
        for k in range(7):
            total = total + factors[k + 1] * zbuf[c][k, :, 0:w].astype(F32)
        ybuf[c][0] = total.astype(BF16)
        for d in YP:
            send(2, c, ybuf[c].at[0], ybuf[c].at[d], (0, 0, d, 0))
        send(2, c, ybuf[c].at[0], ybuf[c].at[0], (0, 0, 0, 0))
        for d in YP:
            send(2, c, ybuf[c].at[0], ybuf[c].at[d], (0, 0, d, 1))

    def stage_in(c):
        s, w = STARTS[c], CHUNKS[c]

        @pl.when(core == 0)
        def _():
            moved(2, c, ybuf[c]).wait_recv()

        @pl.when(core == 1)
        def _():
            moved(2, c, ybuf[c].at[pl.ds(1, 3)]).wait_recv()

        if c == 0:
            win_load.wait()
        rows = ybuf[c][...].reshape(64, w)
        inner = [jnp.dot(rows, win[e, s:s + w, :], preferred_element_type=F32) for e in range(2)]
        if c == 0:
            state["inner"] = inner
        else:
            state["inner"] = [a + b for a, b in zip(state["inner"], inner)]

    def stage_out(c):
        s, w = STARTS[c], CHUNKS[c]
        if c == 0:
            wout_load.wait()
            first = lax.broadcasted_iota(jnp.int32, (64, FS), 0) % 8 < 4
            act = jax.nn.gelu(jnp.where(first, *state["inner"]), approximate=True)
            state["active"] = [
                jnp.where(first, act, 0.0).astype(BF16), jnp.where(first, 0.0, act).astype(BF16)]
        outer = jnp.dot(state["active"][0], wout[0, :, s:s + w], preferred_element_type=F32)
        outer = outer + jnp.dot(state["active"][1], wout[1, :, s:s + w], preferred_element_type=F32)
        rsend[c][...] = outer.reshape(YN, 16, w).astype(BF16)

        @pl.when(core == 0)
        def _():
            for d in YP + (0,):
                send(3, c, rsend[c].at[d], rbuf[c].at[3 + d], (0, 0, YN - d, 1))

        @pl.when(core == 1)
        def _():
            for d in YP:
                send(3, c, rsend[c].at[d], rbuf[c].at[d - 1], (0, 0, YN - d, 1))

    def stage_sum(c):
        w = CHUNKS[c]
        moved(3, c, rbuf[c]).wait_recv()
        total = rsend[c][0].astype(F32)
        for k in range(7):
            total = total + rbuf[c][k].astype(F32)
        agx[c][x, z] = pack(total.reshape(2, 8, w)).astype(BF16)
        for d in ZP:
            send(4, c, agx[c].at[x, z], agx[c].at[x, z], (d, 0, 0, 1))

    def stage_spread(c):
        moved(4, c, agx[c].at[0, pl.ds(0, 7)]).wait_recv()
        for d in XP:
            send(5, c, agx[c].at[x, :, 0], agx[c].at[x, :, 0], (0, d, 0, 0), 6)
            send(5, c, agx[c].at[x, :, 1], agx[c].at[x, :, 1], (0, d, 0, 1))
        send(5, c, agx[c].at[x, :, 0], agx[c].at[x, :, 0], (0, 0, 0, 0), 6)

    def stage_mix(c):
        s, w = STARTS[c], CHUNKS[c]

        @pl.when(core == 0)
        def _():
            moved(5, c, agx[c].at[:, :, 0]).wait_recv()

        @pl.when(core == 1)
        def _():
            moved(5, c, agx[c].at[pl.ds(0, 3), :, 0]).wait_recv()

        rows = [agx[c][xx, :, core].astype(F32) for xx in range(XN)]
        table_ref[:, s:s + w] = jnp.concatenate(
            [jnp.concatenate([rows[xx][zz, :8], rows[xx][zz, 8:]], axis=1)
             for zz in range(ZN) for xx in range(XN)],
            axis=0,
        ).astype(BF16)

    @pl.when(core == 1)
    def _():
        for stage, c in ORDER_IN:
            (stage_x, stage_z)[stage](c)

    for c in range(NC):
        stage_in(c)
    for c in range(NC):
        stage_out(c)

    @pl.when(core == 1)
    def _():
        for stage, c in ORDER_OUT:
            (stage_sum, stage_spread)[stage](c)

    for c in range(NC):
        stage_mix(c)

    @pl.when(core == 0)
    def _():
        for c in range(NC):
            moved(0, c, xbuf[c].at[pl.ds(0, 4)]).wait_send()
            moved(3, c, rbuf[c].at[pl.ds(0, 4)]).wait_send()

    @pl.when(core == 1)
    def _():
        for c in range(NC):
            moved(0, c, xbuf[c].at[pl.ds(0, 3)]).wait_send()
            moved(1, c, zbuf[c]).wait_send()
            moved(2, c, rbuf[c]).wait_send()
            moved(3, c, rbuf[c].at[pl.ds(0, 3)]).wait_send()
            moved(4, c, agx[c].at[0, pl.ds(0, 7)]).wait_send()
            moved(5, c, agx[c].at[pl.ds(0, 3), :, 0]).wait_send()
            moved(6, c, agx[c].at[:, :, 0]).wait_send()


def local(tokens, slot_weight, pattern, w_in, w_out):
    def vm(*shape):
        return pltpu.VMEM(shape, BF16)

    ext = [EXT if c == 0 else 0 for c in range(NC)]
    scratch = [
        vm(TOK, D), vm(D, SLOTS_ALL), pltpu.SMEM((4, 16), jnp.int32),
        vm(2, D, FS), vm(2, FS, D), vm(SLOTS_ALL, TOK)]
    scratch += [vm(SLOTS_ALL, w + e) for w, e in zip(CHUNKS, ext)]
    scratch += [vm(7, 64, w + e) for w, e in zip(CHUNKS, ext)]
    scratch += [vm(ZN, 16, w + e) for w, e in zip(CHUNKS, ext)]
    scratch += [vm(7, 16, w + e) for w, e in zip(CHUNKS, ext)]
    scratch += [vm(YN, 16, w) for w in CHUNKS]
    scratch += [vm(YN, 16, w) for w in CHUNKS]
    scratch += [vm(7, 16, w) for w in CHUNKS]
    scratch += [vm(XN, ZN, 2, 16, w // 2) for w in CHUNKS]
    scratch += [
        pltpu.SemaphoreType.DMA((8,)),
        pltpu.SemaphoreType.DMA((7, NC)), pltpu.SemaphoreType.DMA((6, NC)),
    ]
    hbm = pl.BlockSpec(memory_space=pltpu.HBM)
    vmem = pl.BlockSpec(memory_space=pltpu.VMEM)
    probs, table = pl.pallas_call(
        kernel,
        out_shape=(
            jax.ShapeDtypeStruct((TOK, SLOTS_ALL), BF16),
            jax.ShapeDtypeStruct((SLOTS_ALL, D), BF16),
        ),
        in_specs=[hbm, hbm, hbm, hbm, hbm],
        out_specs=(vmem, vmem),
        scratch_shapes=scratch,
        compiler_params=pltpu.CompilerParams(
            collective_id=0, has_side_effects=True, vmem_limit_bytes=53 << 20),
        name="layer",
    )(tokens.reshape(TOK, D), slot_weight, pattern, w_in, w_out)
    mixed = jnp.dot(probs, table, preferred_element_type=F32).astype(BF16)
    return mixed.reshape(tokens.shape)


def solution(mesh):
    in_specs = (
        P("clip", "seq", None),
        P(),
        P("seq", None),
        P("seq", None, "clip"),
        P("seq", "clip", None),
    )
    return jax.shard_map(
        local, mesh=mesh, in_specs=in_specs, out_specs=P("clip", "seq", None), check_vma=False)
```

```python
import jax
import jax.numpy as jnp
from jax import lax
from jax.experimental import pallas as pl
from jax.experimental.pallas import tpu as pltpu
from jax.sharding import PartitionSpec as P

MESH = pl.DeviceIdType.MESH
BF16, F32 = jnp.bfloat16, jnp.float32
D = 1280
FS = 640
TOK = 512
SLOTS_ALL = 256
ZN, XN, YN = 8, 4, 4
EXT = 128
IN = (256, 512, 256, 256)
IN_AT = tuple(sum(IN[:i]) for i in range(len(IN)))
OUT = (256, 256, 512, 256)
OUT_AT = tuple(sum(OUT[:i]) for i in range(len(OUT)))
NC = 3
ORDER = (0, 1, NC, 2)
RING = (0, 1, 7, 2, 6, 3, 5, 4)
FAR_FIRST = (7, 5, 6, 4, 3, 1, 2)
HALF = 4
NEAR = 5
(X_NEAR, X_FAR, Z_IN, SHARE, REDUCE, Z_NEAR, Z_FAR, S_NEAR, S_FAR, S_OWN) = range(10)
PARTS = {S_OWN: (0, 1), S_NEAR: (1, NEAR - 1), S_FAR: (NEAR, ZN - NEAR)}
LOW = -1.0e30
EMPTY = -1.0e29

XP = (2, 1, 3)
ZP = (4, 3, 5, 2, 6, 1, 7)
YP = (2, 1, 3)


def groups():
    recv, sent = {}, {}
    for c in range(NC + 1):
        for stage in range(S_OWN):
            if c < NC or stage not in (X_FAR, Z_FAR, S_FAR):
                recv[stage, c] = len(recv)
        recv[S_OWN, c] = recv[S_NEAR, c]
        for stage in range(S_OWN + 1):
            if stage in (SHARE, REDUCE):
                sent[stage, c] = 2
            elif c == NC:
                sent[stage, c] = 3 if stage == S_NEAR else 1
            else:
                sent[stage, c] = 0 if stage < SHARE else 3
    return recv, sent


RECV, SENT = groups()
RECV_COUNT = max(RECV.values()) + 1
WA, WB = sum(IN[:NC]) + EXT, IN[NC] + EXT
OA, OB = sum(OUT[:NC]), OUT[NC]
SENT_ALL = (
    ((256, WA), (256, WB), (64, D)),
    ((3 * 64 + 7 * 16, WA), (7 * 32 + 3 * 16 + 48 * OB // WB, WB), (160, D),
     ((7 * 80 * OA + 15 * 32 * OB) // D, D)),
)


def pieces(v):
    hi = v.astype(BF16).astype(F32)
    mid = (v - hi).astype(BF16).astype(F32)
    lo = ((v - hi) - mid).astype(BF16).astype(F32)
    return hi, mid, lo


def ext_of(top, mass):
    lane = lax.broadcasted_iota(jnp.int32, (top.shape[0], EXT), 1)
    out = jnp.zeros((top.shape[0], EXT), F32)
    for i, piece in enumerate(pieces(top) + pieces(mass)):
        out = jnp.where(lane == i, piece, out)
    return out


def of_ext(ext):
    e = ext.astype(F32)
    return e[:, 0:1] + e[:, 1:2] + e[:, 2:3], e[:, 3:4] + e[:, 4:5] + e[:, 5:6]


def merge(stats):
    top = stats[0][0]
    for t, _ in stats[1:]:
        top = jnp.maximum(top, t)
    factors = [jnp.exp(t - top) for t, _ in stats]
    mass = factors[0] * stats[0][1]
    for f, (_, m) in zip(factors[1:], stats[1:]):
        mass = mass + f * m
    return factors, top, mass


def pack(v):
    h = v.shape[-1] // 2
    return jnp.concatenate([v[:, :, :h], v[:, :, h:]], axis=1)


def regroup(v):
    return jnp.concatenate(
        [v[(xx * ZN + p) * 8:(xx * ZN + p) * 8 + 8] for p in range(ZN) for xx in range(XN)],
        axis=0,
    )


def weigh(factors, parts):
    total = factors[0] * parts[0].astype(F32)
    for f, p in zip(factors[1:], parts[1:]):
        total = total + f * p.astype(F32)
    return total


def kernel(tok_hbm, sw_hbm, pat_hbm, win_hbm, wout_hbm, mixed, *scratch):
    it = iter(scratch)
    tok, sw, pat, win, wout, turned, wt_ref, probs, table_ref = (next(it) for _ in range(9))
    psend, xbuf, zsend, zbuf = ([next(it) for _ in range(NC)] for _ in range(4))
    ybuf, rsend, rbuf = ([next(it) for _ in range(NC + 1)] for _ in range(3))
    agx = [next(it) for _ in range(NC)]
    qsend, qbuf, rsx, rbx, agz = (next(it) for _ in range(5))
    load_sem, send_sem, recv_sem = next(it), next(it), next(it)

    seq, clip = lax.axis_index("seq"), lax.axis_index("clip")
    z, x = seq // XN, seq % XN
    y, core = clip // 2, clip % 2

    def dev(dz, dx, dy, k):
        return {
            "seq": ((z + dz) % ZN) * XN + (x + dx) % XN, "clip": ((y + dy) % YN) * 2 + k}

    loads = [
        pltpu.make_async_copy(src, dst, load_sem.at[i])
        for i, (src, dst) in enumerate((
            (sw_hbm, sw), (tok_hbm, tok), (pat_hbm, pat), (win_hbm, win), (wout_hbm, wout)))
    ]
    for load in loads[:3]:
        load.start()

    barrier = pltpu.get_barrier_semaphore()

    def greet(*to):
        pl.semaphore_signal(barrier, inc=1, device_id=dev(*to), device_id_type=MESH)

    for d in XP:
        greet(0, d, 0, 1)
    for d in YP:
        greet(0, 0, d, 1)
    for d in RING[1:]:
        greet(d, 0, 0, 1)

    @pl.when(core == 0)
    def _():
        greet(0, 0, 0, 1)

    @pl.when(core == 1)
    def _():
        greet(0, 0, 0, 0)
        for d in XP:
            greet(0, d, 0, 0)
        for d in YP:
            greet(0, 0, d, 0)
        for d in RING[1:]:
            greet(d, 0, 0, 0)

    def send(stage, c, src, dst, to):
        pltpu.make_async_remote_copy(
            src_ref=src, dst_ref=dst, send_sem=send_sem.at[SENT[stage, c]],
            recv_sem=recv_sem.at[RECV[stage, c]], device_id=dev(*to), device_id_type=MESH,
        ).start()

    def moved(stage, c, view):
        return pltpu.make_async_remote_copy(
            src_ref=view, dst_ref=view, send_sem=send_sem.at[SENT[stage, c]],
            recv_sem=recv_sem.at[RECV[stage, c]], device_id=dev(0, 1, 0, 1),
            device_id_type=MESH,
        )

    def drain(k):
        for i, (rows, lanes) in enumerate(SENT_ALL[k]):
            view = wout.at[pl.ds(0, rows), pl.ds(0, lanes)]
            pltpu.make_async_remote_copy(
                src_ref=view, dst_ref=view, send_sem=send_sem.at[i], recv_sem=recv_sem.at[0],
                device_id=dev(0, 1, 0, 1), device_id_type=MESH,
            ).wait_send()

    loads[0].wait()
    loads[1].wait()
    logits = jnp.dot(tok[...], sw[...], preferred_element_type=F32)
    loads[3].start()
    loads[4].start()
    loads[2].wait()
    group = lax.broadcasted_iota(jnp.int32, (1, SLOTS_ALL), 1) // 4
    masked = []
    for b in range(4):
        named = group == pat[b, 0]
        for j in range(1, 16):
            named = jnp.logical_or(named, group == pat[b, j])
        masked.append(jnp.where(named, logits[b * 128:(b + 1) * 128], LOW))
    turned[...] = jnp.concatenate(masked, axis=0).T
    places = [(z + d) % ZN for d in RING]
    rows = jnp.concatenate(
        [turned[pl.ds(pl.multiple_of(zz * 32 + xx * 8, 8), 8), :]
         for xx in range(XN) for zz in places],
        axis=0,
    )
    top = jnp.maximum(jnp.max(rows, axis=1, keepdims=True), EMPTY)
    weights = jnp.exp(rows - top)
    mass = jnp.sum(weights, axis=1, keepdims=True)
    wt_ref[...] = weights.astype(BF16)
    ext = ext_of(top, mass)
    psend[0][:, IN[0]:] = ext.astype(BF16)
    qsend[:, IN[NC]:] = regroup(ext).astype(BF16)

    def send_x(stage, c):
        at = 32 if stage == X_FAR else 0
        part = pl.ds(at, 32)

        def rows(d):
            return psend[c].at[pl.ds(pl.multiple_of(((x + d) % XN) * 64 + at, 32), 32)]

        @pl.when(core == 0)
        def _():
            for d in XP + (0,):
                send(stage, c, rows(d), xbuf[c].at[3 + d, part], (0, d, 0, 1))

        @pl.when(core == 1)
        def _():
            for d in XP:
                send(stage, c, rows(d), xbuf[c].at[d - 1, part], (0, d, 0, 1))

    for c in range(NC):
        s, w = IN_AT[c], IN[c]
        part = jnp.dot(wt_ref[...], tok[:, s:s + w], preferred_element_type=F32)
        psend[c][:, 0:w] = part.astype(BF16)
        if c == 0:
            @pl.when(core == 0)
            def _():
                pl.semaphore_wait(barrier, 14)

            @pl.when(core == 1)
            def _():
                pl.semaphore_wait(barrier, 27)

        send_x(X_FAR, c)
        if c == 0:
            send_x(X_NEAR, c)
            part = jnp.dot(wt_ref[...], tok[:, IN_AT[NC]:], preferred_element_type=F32)
            qsend[:, 0:IN[NC]] = regroup(part).astype(BF16)

            @pl.when(core == 0)
            def _():
                for p in FAR_FIRST + (0,):
                    send(X_NEAR, NC, qsend.at[pl.ds(32 * p, 32)], qbuf.at[7 + p],
                         (RING[p], 0, 0, 1))

            @pl.when(core == 1)
            def _():
                for p in FAR_FIRST:
                    send(X_NEAR, NC, qsend.at[pl.ds(32 * p, 32)], qbuf.at[p - 1],
                         (RING[p], 0, 0, 1))

    for c in range(1, NC):
        send_x(X_NEAR, c)

    e = jnp.exp(logits - jnp.max(logits, axis=1, keepdims=True))
    probs[...] = (e / jnp.sum(e, axis=1, keepdims=True)).astype(BF16)

    state = {}

    def stage_x(stage, c):
        w = IN[c]
        at = 32 if stage == X_FAR else 0
        half = pl.ds(at // 8, HALF)
        part = slice(at, at + 32)
        mine = pl.ds(pl.multiple_of(x * 64 + at, 32), 32)
        moved(stage, c, xbuf[c].at[:, pl.ds(at, 32)]).wait_recv()

        def sources(lanes):
            return (
                [xbuf[c][k, part, lanes] for k in range(3, 7)],
                [psend[c][mine, lanes]] + [xbuf[c][k, part, lanes] for k in range(3)],
            )

        if c == 0:
            state[stage] = [merge([of_ext(e) for e in exts]) for exts in sources(slice(w, w + EXT))]
            exts = [ext_of(t, m).reshape(HALF, 8, EXT) for _, t, m in state[stage]]
            zsend[0][half, :, w:] = jnp.concatenate(exts, axis=1).astype(BF16)
        totals = [
            weigh(factors, parts).reshape(HALF, 8, w)
            for (factors, _, _), parts in zip(state[stage], sources(slice(0, w)))
        ]
        zsend[c][half, :, 0:w] = jnp.concatenate(totals, axis=1).astype(BF16)
        for p in FAR_FIRST:
            if (p >= HALF) == (stage == X_FAR):
                send(Z_IN, c, zsend[c].at[p], zbuf[c].at[p - 1], (RING[p], 0, 0, 1))

    def stage_z(c):
        w = IN[c]
        moved(Z_IN, c, zbuf[c]).wait_recv()
        if c == 0:
            exts = [zsend[0][0, :, w:]] + [zbuf[0][k, :, w:] for k in range(7)]
            factors, _, mass = merge([of_ext(e) for e in exts])
            state["z"] = [f / mass for f in factors]
        parts = [zsend[c][0, :, 0:w]] + [zbuf[c][k, :, 0:w] for k in range(7)]
        share(c, weigh(state["z"], parts))

    def stage_qz():
        w = IN[NC]
        moved(X_NEAR, NC, qbuf).wait_recv()
        merged, totals = [], []
        for parts in (
            [qbuf[k] for k in range(7, 15)],
            [qsend[0:32, :]] + [qbuf[k] for k in range(7)],
        ):
            factors, top, mass = merge([of_ext(p[:, w:]) for p in parts])
            merged.append(ext_of(top, mass).reshape(XN, 8, EXT))
            totals.append(weigh(factors, [p[:, 0:w] for p in parts]).reshape(XN, 8, w))
        rsx[:, :, 0:w] = jnp.concatenate(totals, axis=1).astype(BF16)
        rsx[:, :, w:] = jnp.concatenate(merged, axis=1).astype(BF16)
        for d in XP:
            send(Z_IN, NC, rsx.at[(x + d) % XN], rbx.at[d - 1], (0, d, 0, 1))

    def stage_qx():
        w = IN[NC]
        moved(Z_IN, NC, rbx).wait_recv()
        parts = [rsx[x]] + [rbx[k] for k in range(3)]
        factors, _, mass = merge([of_ext(p[:, w:]) for p in parts])
        share(NC, weigh([f / mass for f in factors], [p[:, 0:w] for p in parts]))

    def share(c, total):
        ybuf[c][0] = total.astype(BF16)
        for d in YP:
            send(SHARE, c, ybuf[c].at[0], ybuf[c].at[d], (0, 0, d, 0))
        send(SHARE, c, ybuf[c].at[0], ybuf[c].at[0], (0, 0, 0, 0))
        for d in YP:
            send(SHARE, c, ybuf[c].at[0], ybuf[c].at[d], (0, 0, d, 1))

    def stage_in(c):
        s, w = IN_AT[c], IN[c]

        @pl.when(core == 0)
        def _():
            moved(SHARE, c, ybuf[c]).wait_recv()

        @pl.when(core == 1)
        def _():
            moved(SHARE, c, ybuf[c].at[pl.ds(1, 3)]).wait_recv()

        if c == 0:
            loads[3].wait()
        rows = ybuf[c][...].reshape(64, w)
        inner = [jnp.dot(rows, win[e, s:s + w, :], preferred_element_type=F32) for e in range(2)]
        if c == 0:
            state["inner"] = inner
        else:
            state["inner"] = [a + b for a, b in zip(state["inner"], inner)]

    def stage_out(c):
        s, w = OUT_AT[c], OUT[c]
        if c == 0:
            loads[4].wait()
            first = lax.broadcasted_iota(jnp.int32, (64, FS), 0) % 8 < 4
            act = jax.nn.gelu(jnp.where(first, *state["inner"]), approximate=True)
            state["active"] = jnp.concatenate(
                [jnp.where(first, act, 0.0), jnp.where(first, 0.0, act)], axis=1).astype(BF16)
        if c < 2:
            lanes = slice(0, OUT[0]) if c == 0 else slice(OUT[0], D)
            state["outer"] = jnp.dot(
                state["active"], wout[:, lanes], preferred_element_type=F32)
            state["at"] = lanes.start
        outer = state["outer"][:, s - state["at"]:s - state["at"] + w]
        rsend[c][...] = outer.reshape(YN, 16, w).astype(BF16)

        @pl.when(core == 0)
        def _():
            for d in YP + (0,):
                send(REDUCE, c, rsend[c].at[d], rbuf[c].at[3 + d], (0, 0, YN - d, 1))

        @pl.when(core == 1)
        def _():
            for d in YP:
                send(REDUCE, c, rsend[c].at[d], rbuf[c].at[d - 1], (0, 0, YN - d, 1))

    def stage_sum(c):
        w = OUT[c]
        moved(REDUCE, c, rbuf[c]).wait_recv()
        total = rsend[c][0].astype(F32)
        for k in range(7):
            total = total + rbuf[c][k].astype(F32)
        total = pack(total.reshape(2, 8, w)).astype(BF16)
        if c == NC:
            agz[z, x] = total
            for d in XP:
                send(Z_NEAR, NC, agz.at[z, x], agz.at[z, x], (0, d, 0, 1))
        else:
            agx[c][x, 0] = total
            for p in range(1, NEAR):
                send(Z_NEAR, c, agx[c].at[x, 0], agx[c].at[x, p], (ZN - RING[p], 0, 0, 1))
            spread(S_OWN, c)
            for p in range(NEAR, ZN):
                send(Z_FAR, c, agx[c].at[x, 0], agx[c].at[x, p], (ZN - RING[p], 0, 0, 1))

    def stage_spread_z():
        moved(Z_NEAR, NC, agz.at[0, pl.ds(0, 3)]).wait_recv()
        for p in FAR_FIRST:
            send(S_NEAR, NC, agz.at[z, :, 0], agz.at[z, :, 0], (RING[p], 0, 0, 0))
            send(S_NEAR, NC, agz.at[z, :, 1], agz.at[z, :, 1], (RING[p], 0, 0, 1))
        send(S_NEAR, NC, agz.at[z, :, 0], agz.at[z, :, 0], (0, 0, 0, 0))

    def stage_near(c):
        moved(Z_NEAR, c, agx[c].at[0, pl.ds(1, NEAR - 1)]).wait_recv()
        spread(S_NEAR, c)

    def stage_far(c):
        moved(Z_FAR, c, agx[c].at[0, pl.ds(NEAR, ZN - NEAR)]).wait_recv()
        spread(S_FAR, c)

    def spread(stage, c):
        places = pl.ds(*PARTS[stage])
        for d in XP:
            part = agx[c].at[x, places, 0]
            send(stage, c, part, part, (0, d, 0, 0))
            part = agx[c].at[x, places, 1]
            send(stage, c, part, part, (0, d, 0, 1))
        part = agx[c].at[x, places, 0]
        send(stage, c, part, part, (0, 0, 0, 0))

    def stage_mix_z():
        @pl.when(core == 0)
        def _():
            moved(S_NEAR, NC, agz.at[:, :, 0]).wait_recv()

        @pl.when(core == 1)
        def _():
            moved(S_NEAR, NC, agz.at[pl.ds(0, 7), :, 0]).wait_recv()

        rows = agz[:, :, core].astype(F32).reshape(ZN * XN, 16, OUT[NC] // 2)
        table_ref[:, OUT_AT[NC]:] = jnp.concatenate(
            [rows[:, :8], rows[:, 8:]], axis=2).reshape(SLOTS_ALL, OUT[NC]).astype(BF16)

    def stage_mix(stage, c):
        s, w = OUT_AT[c], OUT[c]
        first, count = PARTS[stage]
        if stage == S_NEAR:
            first, count = 0, NEAR

        @pl.when(core == 0)
        def _():
            moved(stage, c, agx[c].at[:, pl.ds(first, count), 0]).wait_recv()

        @pl.when(core == 1)
        def _():
            moved(stage, c, agx[c].at[pl.ds(0, 3), pl.ds(first, count), 0]).wait_recv()

        for p in range(first, first + count):
            rows = agx[c][:, p, core].astype(F32)
            at = pl.ds(pl.multiple_of(places[p] * 32, 32), 32)
            table_ref[at, s:s + w] = jnp.concatenate(
                [rows[:, :8], rows[:, 8:]], axis=2).reshape(32, w).astype(BF16)

    @pl.when(core == 1)
    def _():
        stage_x(X_FAR, 0)
        stage_x(X_NEAR, 0)
        stage_x(X_FAR, 1)
        stage_x(X_FAR, 2)
        stage_x(X_NEAR, 1)
        stage_z(0)
        stage_x(X_NEAR, 2)
        stage_qz()
        stage_z(1)
        stage_qx()
        stage_z(2)

    for c in ORDER:
        stage_in(c)
    for c in ORDER:
        stage_out(c)

    @pl.when(core == 1)
    def _():
        for c in ORDER:
            stage_sum(c)
        stage_near(0)
        stage_near(1)
        stage_spread_z()
        stage_far(0)
        stage_near(2)
        stage_far(1)
        stage_far(2)

    stage_mix(S_NEAR, 0)
    stage_mix(S_NEAR, 1)

    def finish(c):
        lanes = slice(OUT_AT[c], OUT_AT[c] + OUT[c])
        mixed[:, lanes] = jnp.dot(
            probs[...], table_ref[:, lanes], preferred_element_type=F32).astype(BF16)

    stage_mix(S_FAR, 0)
    finish(0)
    stage_mix_z()
    finish(NC)
    stage_mix(S_NEAR, 2)
    stage_mix(S_FAR, 1)
    finish(1)
    stage_mix(S_FAR, 2)
    finish(2)

    @pl.when(core == 0)
    def _():
        drain(0)

    @pl.when(core == 1)
    def _():
        drain(1)


def local(tokens, slot_weight, pattern, w_in, w_out):
    def vm(*shape):
        return pltpu.VMEM(shape, BF16)

    first = [w + (EXT if c == 0 else 0) for c, w in enumerate(IN[:NC])]
    scratch = [
        vm(TOK, D), vm(D, SLOTS_ALL), pltpu.SMEM((4, 16), jnp.int32),
        vm(2, D, FS), vm(2 * FS, D), pltpu.VMEM((SLOTS_ALL, TOK), F32), vm(SLOTS_ALL, TOK),
        vm(TOK, SLOTS_ALL), vm(SLOTS_ALL, D)]
    scratch += [vm(SLOTS_ALL, w) for w in first]
    scratch += [vm(7, 64, w) for w in first]
    scratch += [vm(ZN, 16, w) for w in first]
    scratch += [vm(7, 16, w) for w in first]
    scratch += [vm(YN, 16, w) for w in IN]
    scratch += [vm(YN, 16, w) for w in OUT]
    scratch += [vm(7, 16, w) for w in OUT]
    scratch += [vm(XN, ZN, 2, 16, w // 2) for w in OUT[:NC]]
    last = IN[NC] + EXT
    scratch += [
        vm(SLOTS_ALL, last), vm(15, 32, last), vm(XN, 16, last), vm(3, 16, last),
        vm(ZN, XN, 2, 16, OUT[NC] // 2),
        pltpu.SemaphoreType.DMA((5,)),
        pltpu.SemaphoreType.DMA((4,)), pltpu.SemaphoreType.DMA((RECV_COUNT,)),
    ]
    arrays = (tokens.reshape(TOK, D), slot_weight, pattern, w_in, w_out.reshape(2 * FS, D))
    hbm = pl.BlockSpec(memory_space=pltpu.HBM)
    vmem = pl.BlockSpec(memory_space=pltpu.VMEM)
    mixed = pl.pallas_call(
        kernel,
        out_shape=pltpu.VMEM((TOK, D), BF16),
        in_specs=[hbm, hbm, hbm, hbm, hbm],
        out_specs=vmem,
        scratch_shapes=scratch,
        compiler_params=pltpu.CompilerParams(
            collective_id=0, has_side_effects=True, vmem_limit_bytes=40 << 20),
        name="layer",
    )(*(pltpu.with_memory_space_constraint(a, pltpu.HBM) for a in arrays))
    return mixed.reshape(tokens.shape)


def solution(mesh):
    in_specs = (
        P("clip", "seq", None),
        P(),
        P("seq", None),
        P("seq", None, "clip"),
        P("seq", "clip", None),
    )
    return jax.shard_map(
        local, mesh=mesh, in_specs=in_specs, out_specs=P("clip", "seq", None), check_vma=False)
```

```python
import jax
import jax.numpy as jnp
from jax import lax
from jax.experimental import pallas as pl
from jax.experimental.pallas import tpu as pltpu
from jax.sharding import PartitionSpec as P

MESH = pl.DeviceIdType.MESH
BF16, F32 = jnp.bfloat16, jnp.float32
D = 1280
FS = 640
TOK = 512
SLOTS_ALL = 256
ZN, XN, YN = 8, 4, 4
EXT = 128
IN = (256, 512, 256, 256)
IN_AT = tuple(sum(IN[:i]) for i in range(len(IN)))
OUT = (256, 256, 512, 256)
OUT_AT = tuple(sum(OUT[:i]) for i in range(len(OUT)))
NC = 3
ORDER = (0, 1, NC, 2)
RING = (0, 1, 7, 2, 6, 3, 5, 4)
FAR_FIRST = (7, 5, 6, 4, 3, 1, 2)
HALF = 4
NEAR = 5
(X_NEAR, X_FAR, Z_IN, SHARE, REDUCE, Z_NEAR, Z_FAR, S_NEAR, S_FAR, S_OWN, STATS) = range(11)
PARTS = {S_OWN: (0, 1), S_NEAR: (1, NEAR - 1), S_FAR: (NEAR, ZN - NEAR)}
LOW = -1.0e30
EMPTY = -1.0e29

XP = (2, 1, 3)
ZP = (4, 3, 5, 2, 6, 1, 7)
YP = (2, 1, 3)


def groups():
    recv, sent = {}, {}
    for c in range(NC + 1):
        for stage in range(S_OWN):
            if c < NC or stage not in (X_FAR, Z_FAR, S_FAR):
                recv[stage, c] = len(set(recv.values()))
        recv[S_OWN, c] = recv[S_NEAR, c]
        if c in (0, NC):
            recv[STATS, c] = len(set(recv.values()))
        for stage in range(STATS + 1):
            if stage in (SHARE, REDUCE):
                sent[stage, c] = 2
            elif c == NC:
                sent[stage, c] = 3 if stage == S_NEAR else 1
            else:
                sent[stage, c] = 0 if stage < SHARE or stage == STATS else 3
    return recv, sent


RECV, SENT = groups()
RECV_COUNT = max(RECV.values()) + 1
WA, OA = sum(IN[:NC]), sum(OUT[:NC])
WB, OB = IN[NC], OUT[NC]
SENT_ALL = (
    (4 * 4 * WA // 128 + 4, 8 * 2 * WB // 128 + 8, 4 * D // 128),
    (3 * 4 * WA // 128 + 3 + 7 * (WA + EXT) // 128,
     7 * 2 * WB // 128 + 7 + 3 * (WB + EXT) // 128 + 3 * OB // 128,
     10 * D // 128,
     (7 * 5 * OA + 15 * 2 * OB) // 128),
)


def pieces(v):
    hi = v.astype(BF16).astype(F32)
    mid = (v - hi).astype(BF16).astype(F32)
    lo = ((v - hi) - mid).astype(BF16).astype(F32)
    return hi, mid, lo


def ext_of(top, mass):
    lane = lax.broadcasted_iota(jnp.int32, (top.shape[0], EXT), 1)
    out = jnp.zeros((top.shape[0], EXT), F32)
    for i, piece in enumerate(pieces(top) + pieces(mass)):
        out = jnp.where(lane == i, piece, out)
    return out


def of_ext(ext):
    e = ext.astype(F32)
    return e[:, 0:1] + e[:, 1:2] + e[:, 2:3], e[:, 3:4] + e[:, 4:5] + e[:, 5:6]


def as_tiles(ext):
    t = ext.T[:16]
    return jnp.stack([t[:, :128], t[:, 128:]]).astype(BF16)


def of_tiles(tiles):
    return tiles.reshape(-1, 128).astype(F32).T


def merge(stats):
    top = stats[0][0]
    for t, _ in stats[1:]:
        top = jnp.maximum(top, t)
    factors = [jnp.exp(t - top) for t, _ in stats]
    mass = factors[0] * stats[0][1]
    for f, (_, m) in zip(factors[1:], stats[1:]):
        mass = mass + f * m
    return factors, top, mass


def pack(v):
    h = v.shape[-1] // 2
    return jnp.concatenate([v[:, :, :h], v[:, :, h:]], axis=1)


def regroup(v):
    return jnp.concatenate(
        [v[(xx * ZN + p) * 8:(xx * ZN + p) * 8 + 8] for p in range(ZN) for xx in range(XN)],
        axis=0,
    )


def weigh(factors, parts):
    total = factors[0] * parts[0].astype(F32)
    for f, p in zip(factors[1:], parts[1:]):
        total = total + f * p.astype(F32)
    return total


def kernel(tok_hbm, sw_hbm, pat_hbm, win_hbm, wout_hbm, mixed, *scratch):
    it = iter(scratch)
    tok, sw, pat, win, wout, turned, wt_ref, probs, table_ref = (next(it) for _ in range(9))
    psend, xbuf, zsend, zbuf = ([next(it) for _ in range(NC)] for _ in range(4))
    ybuf, rsend, rbuf = ([next(it) for _ in range(NC + 1)] for _ in range(3))
    agx = [next(it) for _ in range(NC)]
    qsend, qbuf, rsx, rbx, agz, xstat, xstats, qstat, qstats, yard = (next(it) for _ in range(10))
    load_sem, send_sem, recv_sem = next(it), next(it), next(it)

    seq, clip = lax.axis_index("seq"), lax.axis_index("clip")
    z, x = seq // XN, seq % XN
    y, core = clip // 2, clip % 2

    def dev(dz, dx, dy, k):
        return {
            "seq": ((z + dz) % ZN) * XN + (x + dx) % XN, "clip": ((y + dy) % YN) * 2 + k}

    loads = [
        pltpu.make_async_copy(src, dst, load_sem.at[i])
        for i, (src, dst) in enumerate((
            (sw_hbm, sw), (tok_hbm, tok), (pat_hbm, pat), (win_hbm, win), (wout_hbm, wout)))
    ]
    for load in loads[:3]:
        load.start()

    barrier = pltpu.get_barrier_semaphore()

    def greet(*to):
        pl.semaphore_signal(barrier, inc=1, device_id=dev(*to), device_id_type=MESH)

    for d in XP:
        greet(0, d, 0, 1)
    for d in YP:
        greet(0, 0, d, 1)
    for d in RING[1:]:
        greet(d, 0, 0, 1)

    @pl.when(core == 0)
    def _():
        greet(0, 0, 0, 1)

    @pl.when(core == 1)
    def _():
        greet(0, 0, 0, 0)
        for d in XP:
            greet(0, d, 0, 0)
        for d in YP:
            greet(0, 0, d, 0)
        for d in RING[1:]:
            greet(d, 0, 0, 0)

    def send(stage, c, src, dst, to):
        pltpu.make_async_remote_copy(
            src_ref=src, dst_ref=dst, send_sem=send_sem.at[SENT[stage, c]],
            recv_sem=recv_sem.at[RECV[stage, c]], device_id=dev(*to), device_id_type=MESH,
        ).start()

    def moved(stage, c, view):
        return pltpu.make_async_remote_copy(
            src_ref=view, dst_ref=view, send_sem=send_sem.at[SENT[stage, c]],
            recv_sem=recv_sem.at[RECV[stage, c]], device_id=dev(0, 1, 0, 1),
            device_id_type=MESH,
        )

    def drain(k):
        for i, tiles in enumerate(SENT_ALL[k]):
            view = yard.at[pl.ds(0, tiles)]
            pltpu.make_async_remote_copy(
                src_ref=view, dst_ref=view, send_sem=send_sem.at[i], recv_sem=recv_sem.at[0],
                device_id=dev(0, 1, 0, 1), device_id_type=MESH,
            ).wait_send()

    loads[0].wait()
    loads[1].wait()
    logits = jnp.dot(tok[...], sw[...], preferred_element_type=F32)
    loads[3].start()
    loads[4].start()
    loads[2].wait()
    group = lax.broadcasted_iota(jnp.int32, (1, SLOTS_ALL), 1) // 4
    masked = []
    for b in range(4):
        named = group == pat[b, 0]
        for j in range(1, 16):
            named = jnp.logical_or(named, group == pat[b, j])
        masked.append(jnp.where(named, logits[b * 128:(b + 1) * 128], LOW))
    turned[...] = jnp.concatenate(masked, axis=0).T
    places = [(z + d) % ZN for d in RING]
    rows = jnp.concatenate(
        [turned[pl.ds(pl.multiple_of(zz * 32 + xx * 8, 8), 8), :]
         for xx in range(XN) for zz in places],
        axis=0,
    )
    top = jnp.maximum(jnp.max(rows, axis=1, keepdims=True), EMPTY)
    weights = jnp.exp(rows - top)
    mass = jnp.sum(weights, axis=1, keepdims=True)
    wt_ref[...] = weights.astype(BF16)
    ext = ext_of(top, mass)

    def send_x(stage, c):
        at = 32 if stage == X_FAR else 0
        part = pl.ds(at, 32)

        def rows(d):
            return psend[c].at[pl.ds(pl.multiple_of(((x + d) % XN) * 64 + at, 32), 32)]

        @pl.when(core == 0)
        def _():
            for d in XP + (0,):
                send(stage, c, rows(d), xbuf[c].at[3 + d, part], (0, d, 0, 1))

        @pl.when(core == 1)
        def _():
            for d in XP:
                send(stage, c, rows(d), xbuf[c].at[d - 1, part], (0, d, 0, 1))

    for c in range(NC):
        s, w = IN_AT[c], IN[c]
        part = jnp.dot(wt_ref[...], tok[:, s:s + w], preferred_element_type=F32)
        psend[c][:, 0:w] = part.astype(BF16)
        if c == 0:
            @pl.when(core == 0)
            def _():
                pl.semaphore_wait(barrier, 14)

            @pl.when(core == 1)
            def _():
                pl.semaphore_wait(barrier, 27)

        send_x(X_FAR, c)
        if c == 0:
            send_x(X_NEAR, c)
            xstat[...] = as_tiles(ext)
            qstat[...] = as_tiles(regroup(ext))

            @pl.when(core == 0)
            def _():
                for d in XP + (0,):
                    send(STATS, 0, xstat.at[(x + d) % XN // 2], xstats.at[3 + d], (0, d, 0, 1))
                for p in FAR_FIRST + (0,):
                    send(STATS, NC, qstat.at[p // 4], qstats.at[7 + p], (RING[p], 0, 0, 1))

            @pl.when(core == 1)
            def _():
                for d in XP:
                    send(STATS, 0, xstat.at[(x + d) % XN // 2], xstats.at[d - 1], (0, d, 0, 1))
                for p in FAR_FIRST:
                    send(STATS, NC, qstat.at[p // 4], qstats.at[p - 1], (RING[p], 0, 0, 1))

            part = jnp.dot(wt_ref[...], tok[:, IN_AT[NC]:], preferred_element_type=F32)
            qsend[...] = regroup(part).astype(BF16)

            @pl.when(core == 0)
            def _():
                for p in FAR_FIRST + (0,):
                    send(X_NEAR, NC, qsend.at[pl.ds(32 * p, 32)], qbuf.at[7 + p],
                         (RING[p], 0, 0, 1))

            @pl.when(core == 1)
            def _():
                for p in FAR_FIRST:
                    send(X_NEAR, NC, qsend.at[pl.ds(32 * p, 32)], qbuf.at[p - 1],
                         (RING[p], 0, 0, 1))

    for c in range(1, NC):
        send_x(X_NEAR, c)

    e = jnp.exp(logits - jnp.max(logits, axis=1, keepdims=True))
    probs[...] = (e / jnp.sum(e, axis=1, keepdims=True)).astype(BF16)

    state = {}

    def stage_x(stage, c):
        w = IN[c]
        at = 32 if stage == X_FAR else 0
        half = pl.ds(at // 8, HALF)
        part = slice(at, at + 32)
        mine = pl.ds(pl.multiple_of(x * 64 + at, 32), 32)
        moved(stage, c, xbuf[c].at[:, pl.ds(at, 32)]).wait_recv()

        sources = (
            [xbuf[c][k, part] for k in range(3, 7)],
            [psend[c][mine]] + [xbuf[c][k, part] for k in range(3)],
        )
        if c == 0 and stage == X_FAR:
            moved(STATS, 0, xstats).wait_recv()
            t = of_tiles(jnp.concatenate([xstats[...], xstat[x // 2][None]]))
            t = jnp.where(x % 2 == 0, t[:64], t[64:])
            state["stats"] = [t[:, 16 * k:16 * k + 16] for k in (3, 4, 5, 6, 7, 0, 1, 2)]
        if c == 0:
            stats = [of_ext(t[part]) for t in state["stats"]]
            state[stage] = [merge(stats[:4]), merge(stats[4:])]
            exts = [ext_of(t, m).reshape(HALF, 8, EXT) for _, t, m in state[stage]]
            zsend[0][half, :, w:] = jnp.concatenate(exts, axis=1).astype(BF16)
        totals = [
            weigh(factors, parts).reshape(HALF, 8, w)
            for (factors, _, _), parts in zip(state[stage], sources)
        ]
        zsend[c][half, :, 0:w] = jnp.concatenate(totals, axis=1).astype(BF16)
        for p in FAR_FIRST:
            if (p >= HALF) == (stage == X_FAR):
                send(Z_IN, c, zsend[c].at[p], zbuf[c].at[p - 1], (RING[p], 0, 0, 1))

    def stage_z(c):
        w = IN[c]
        moved(Z_IN, c, zbuf[c]).wait_recv()
        if c == 0:
            exts = [zsend[0][0, :, w:]] + [zbuf[0][k, :, w:] for k in range(7)]
            factors, _, mass = merge([of_ext(e) for e in exts])
            state["z"] = [f / mass for f in factors]
        parts = [zsend[c][0, :, 0:w]] + [zbuf[c][k, :, 0:w] for k in range(7)]
        share(c, weigh(state["z"], parts))

    def stage_qstats():
        moved(STATS, NC, qstats).wait_recv()
        t = of_tiles(jnp.concatenate([qstats[...], qstat[0:1]]))
        stats = [
            of_ext(t[32 * (p % 4):32 * (p % 4) + 32, 16 * k:16 * k + 16])
            for p, k in [(p, 7 + p) for p in range(8)] + [(0, 15)] + [(p, p - 1) for p in range(1, 8)]
        ]
        state["q"] = [merge(stats[:8]), merge(stats[8:])]
        merged = [ext_of(top, mass).reshape(XN, 8, EXT) for _, top, mass in state["q"]]
        rsx[:, :, IN[NC]:] = jnp.concatenate(merged, axis=1).astype(BF16)

    def stage_qz():
        w = IN[NC]
        moved(X_NEAR, NC, qbuf).wait_recv()
        sources = (
            [qbuf[k] for k in range(7, 15)],
            [qsend[0:32, :]] + [qbuf[k] for k in range(7)],
        )
        totals = [
            weigh(factors, parts).reshape(XN, 8, w)
            for (factors, _, _), parts in zip(state["q"], sources)
        ]
        rsx[:, :, 0:w] = jnp.concatenate(totals, axis=1).astype(BF16)
        for d in XP:
            send(Z_IN, NC, rsx.at[(x + d) % XN], rbx.at[d - 1], (0, d, 0, 1))

    def stage_qx():
        w = IN[NC]
        moved(Z_IN, NC, rbx).wait_recv()
        parts = [rsx[x]] + [rbx[k] for k in range(3)]
        factors, _, mass = merge([of_ext(p[:, w:]) for p in parts])
        share(NC, weigh([f / mass for f in factors], [p[:, 0:w] for p in parts]))

    def share(c, total):
        ybuf[c][0] = total.astype(BF16)
        for d in YP:
            send(SHARE, c, ybuf[c].at[0], ybuf[c].at[d], (0, 0, d, 0))
        send(SHARE, c, ybuf[c].at[0], ybuf[c].at[0], (0, 0, 0, 0))
        for d in YP:
            send(SHARE, c, ybuf[c].at[0], ybuf[c].at[d], (0, 0, d, 1))

    def stage_in(c):
        s, w = IN_AT[c], IN[c]

        @pl.when(core == 0)
        def _():
            moved(SHARE, c, ybuf[c]).wait_recv()

        @pl.when(core == 1)
        def _():
            moved(SHARE, c, ybuf[c].at[pl.ds(1, 3)]).wait_recv()

        if c == 0:
            loads[3].wait()
        rows = ybuf[c][...].reshape(64, w)
        inner = [jnp.dot(rows, win[e, s:s + w, :], preferred_element_type=F32) for e in range(2)]
        if c == 0:
            state["inner"] = inner
        else:
            state["inner"] = [a + b for a, b in zip(state["inner"], inner)]

    def stage_out(c):
        s, w = OUT_AT[c], OUT[c]
        if c == 0:
            loads[4].wait()
            first = lax.broadcasted_iota(jnp.int32, (64, FS), 0) % 8 < 4
            act = jax.nn.gelu(jnp.where(first, *state["inner"]), approximate=True)
            state["active"] = jnp.concatenate(
                [jnp.where(first, act, 0.0), jnp.where(first, 0.0, act)], axis=1).astype(BF16)
        if c < 2:
            lanes = slice(0, OUT[0]) if c == 0 else slice(OUT[0], D)
            state["outer"] = jnp.dot(
                state["active"], wout[:, lanes], preferred_element_type=F32)
            state["at"] = lanes.start
        outer = state["outer"][:, s - state["at"]:s - state["at"] + w]
        rsend[c][...] = outer.reshape(YN, 16, w).astype(BF16)

        @pl.when(core == 0)
        def _():
            for d in YP + (0,):
                send(REDUCE, c, rsend[c].at[d], rbuf[c].at[3 + d], (0, 0, YN - d, 1))

        @pl.when(core == 1)
        def _():
            for d in YP:
                send(REDUCE, c, rsend[c].at[d], rbuf[c].at[d - 1], (0, 0, YN - d, 1))

    def stage_sum(c):
        w = OUT[c]
        moved(REDUCE, c, rbuf[c]).wait_recv()
        total = rsend[c][0].astype(F32)
        for k in range(7):
            total = total + rbuf[c][k].astype(F32)
        total = pack(total.reshape(2, 8, w)).astype(BF16)
        if c == NC:
            agz[z, x] = total
            for d in XP:
                send(Z_NEAR, NC, agz.at[z, x], agz.at[z, x], (0, d, 0, 1))
        else:
            agx[c][x, 0] = total
            for p in range(1, NEAR):
                send(Z_NEAR, c, agx[c].at[x, 0], agx[c].at[x, p], (ZN - RING[p], 0, 0, 1))
            spread(S_OWN, c)
            for p in range(NEAR, ZN):
                send(Z_FAR, c, agx[c].at[x, 0], agx[c].at[x, p], (ZN - RING[p], 0, 0, 1))

    def stage_spread_z():
        moved(Z_NEAR, NC, agz.at[0, pl.ds(0, 3)]).wait_recv()
        for p in FAR_FIRST:
            send(S_NEAR, NC, agz.at[z, :, 0], agz.at[z, :, 0], (RING[p], 0, 0, 0))
            send(S_NEAR, NC, agz.at[z, :, 1], agz.at[z, :, 1], (RING[p], 0, 0, 1))
        send(S_NEAR, NC, agz.at[z, :, 0], agz.at[z, :, 0], (0, 0, 0, 0))

    def stage_near(c):
        moved(Z_NEAR, c, agx[c].at[0, pl.ds(1, NEAR - 1)]).wait_recv()
        spread(S_NEAR, c)

    def stage_far(c):
        moved(Z_FAR, c, agx[c].at[0, pl.ds(NEAR, ZN - NEAR)]).wait_recv()
        spread(S_FAR, c)

    def spread(stage, c):
        places = pl.ds(*PARTS[stage])
        for d in XP:
            part = agx[c].at[x, places, 0]
            send(stage, c, part, part, (0, d, 0, 0))
            part = agx[c].at[x, places, 1]
            send(stage, c, part, part, (0, d, 0, 1))
        part = agx[c].at[x, places, 0]
        send(stage, c, part, part, (0, 0, 0, 0))

    def stage_mix_z():
        @pl.when(core == 0)
        def _():
            moved(S_NEAR, NC, agz.at[:, :, 0]).wait_recv()

        @pl.when(core == 1)
        def _():
            moved(S_NEAR, NC, agz.at[pl.ds(0, 7), :, 0]).wait_recv()

        rows = agz[:, :, core].astype(F32).reshape(ZN * XN, 16, OUT[NC] // 2)
        table_ref[:, OUT_AT[NC]:] = jnp.concatenate(
            [rows[:, :8], rows[:, 8:]], axis=2).reshape(SLOTS_ALL, OUT[NC]).astype(BF16)

    def stage_mix(stage, c):
        s, w = OUT_AT[c], OUT[c]
        first, count = PARTS[stage]
        if stage == S_NEAR:
            first, count = 0, NEAR

        @pl.when(core == 0)
        def _():
            moved(stage, c, agx[c].at[:, pl.ds(first, count), 0]).wait_recv()

        @pl.when(core == 1)
        def _():
            moved(stage, c, agx[c].at[pl.ds(0, 3), pl.ds(first, count), 0]).wait_recv()

        for p in range(first, first + count):
            rows = agx[c][:, p, core].astype(F32)
            at = pl.ds(pl.multiple_of(places[p] * 32, 32), 32)
            table_ref[at, s:s + w] = jnp.concatenate(
                [rows[:, :8], rows[:, 8:]], axis=2).reshape(32, w).astype(BF16)

    @pl.when(core == 1)
    def _():
        stage_x(X_FAR, 0)
        stage_x(X_NEAR, 0)
        stage_x(X_FAR, 1)
        stage_x(X_FAR, 2)
        stage_qstats()
        stage_x(X_NEAR, 1)
        stage_x(X_NEAR, 2)
        stage_qz()
        stage_z(0)
        stage_z(1)
        stage_qx()
        stage_z(2)

    for c in ORDER:
        stage_in(c)
    for c in ORDER:
        stage_out(c)

    @pl.when(core == 1)
    def _():
        for c in ORDER:
            stage_sum(c)
        stage_near(0)
        stage_near(1)
        stage_spread_z()
        stage_far(0)
        stage_near(2)
        stage_far(1)
        stage_far(2)

    stage_mix(S_NEAR, 0)
    stage_mix(S_NEAR, 1)

    def finish(c):
        lanes = slice(OUT_AT[c], OUT_AT[c] + OUT[c])
        mixed[:, lanes] = jnp.dot(
            probs[...], table_ref[:, lanes], preferred_element_type=F32).astype(BF16)

    stage_mix(S_FAR, 0)
    finish(0)
    stage_mix_z()
    finish(NC)
    stage_mix(S_NEAR, 2)
    stage_mix(S_FAR, 1)
    finish(1)
    stage_mix(S_FAR, 2)
    finish(2)

    @pl.when(core == 0)
    def _():
        drain(0)

    @pl.when(core == 1)
    def _():
        drain(1)


def local(tokens, slot_weight, pattern, w_in, w_out):
    def vm(*shape):
        return pltpu.VMEM(shape, BF16)

    first = [w + (EXT if c == 0 else 0) for c, w in enumerate(IN[:NC])]
    scratch = [
        vm(TOK, D), vm(D, SLOTS_ALL), pltpu.SMEM((4, 16), jnp.int32),
        vm(2, D, FS), vm(2 * FS, D), pltpu.VMEM((SLOTS_ALL, TOK), F32), vm(SLOTS_ALL, TOK),
        vm(TOK, SLOTS_ALL), vm(SLOTS_ALL, D)]
    scratch += [vm(SLOTS_ALL, w) for w in IN[:NC]]
    scratch += [vm(7, 64, w) for w in IN[:NC]]
    scratch += [vm(ZN, 16, w) for w in first]
    scratch += [vm(7, 16, w) for w in first]
    scratch += [vm(YN, 16, w) for w in IN]
    scratch += [vm(YN, 16, w) for w in OUT]
    scratch += [vm(7, 16, w) for w in OUT]
    scratch += [vm(XN, ZN, 2, 16, w // 2) for w in OUT[:NC]]
    last = IN[NC] + EXT
    scratch += [
        vm(SLOTS_ALL, IN[NC]), vm(15, 32, IN[NC]), vm(XN, 16, last), vm(3, 16, last),
        vm(ZN, XN, 2, 16, OUT[NC] // 2),
        vm(2, 16, 128), vm(7, 16, 128), vm(2, 16, 128), vm(15, 16, 128),
        vm(max(max(tiles) for tiles in SENT_ALL), 16, 128),
        pltpu.SemaphoreType.DMA((5,)),
        pltpu.SemaphoreType.DMA((4,)), pltpu.SemaphoreType.DMA((RECV_COUNT,)),
    ]
    arrays = (tokens.reshape(TOK, D), slot_weight, pattern, w_in, w_out.reshape(2 * FS, D))
    hbm = pl.BlockSpec(memory_space=pltpu.HBM)
    vmem = pl.BlockSpec(memory_space=pltpu.VMEM)
    mixed = pl.pallas_call(
        kernel,
        out_shape=pltpu.VMEM((TOK, D), BF16),
        in_specs=[hbm, hbm, hbm, hbm, hbm],
        out_specs=vmem,
        scratch_shapes=scratch,
        compiler_params=pltpu.CompilerParams(
            collective_id=0, has_side_effects=True, vmem_limit_bytes=40 << 20),
        name="layer",
    )(*(pltpu.with_memory_space_constraint(a, pltpu.HBM) for a in arrays))
    return mixed.reshape(tokens.shape)


def solution(mesh):
    in_specs = (
        P("clip", "seq", None),
        P(),
        P("seq", None),
        P("seq", None, "clip"),
        P("seq", "clip", None),
    )
    return jax.shard_map(
        local, mesh=mesh, in_specs=in_specs, out_specs=P("clip", "seq", None), check_vma=False)
```

```python
import jax
import jax.numpy as jnp
from jax import lax
from jax.experimental import pallas as pl
from jax.experimental.pallas import tpu as pltpu
from jax.sharding import PartitionSpec as P

MESH = pl.DeviceIdType.MESH
BF16, F32 = jnp.bfloat16, jnp.float32
D = 1280
FS = 640
TOK = 512
SLOTS_ALL = 256
ZN, XN, YN = 8, 4, 4
EXT = 128
IN = (256, 512, 256, 256)
IN_AT = tuple(sum(IN[:i]) for i in range(len(IN)))
OUT = (256, 256, 512, 256)
OUT_AT = tuple(sum(OUT[:i]) for i in range(len(OUT)))
NC = 3
ORDER = (0, 1, NC, 2)
RING = (0, 1, 7, 2, 6, 3, 5, 4)
FAR_FIRST = (7, 5, 6, 4, 3, 1, 2)
HALF = 4
NEAR = 5
(X_NEAR, X_FAR, Z_IN, SHARE, REDUCE, Z_NEAR, Z_FAR, S_NEAR, S_FAR, S_OWN, STATS) = range(11)
PARTS = {S_OWN: (0, 1), S_NEAR: (1, NEAR - 1), S_FAR: (NEAR, ZN - NEAR)}
LOW = -1.0e30
EMPTY = -1.0e29

XP = (2, 1, 3)
ZP = (4, 3, 5, 2, 6, 1, 7)
YP = (2, 1, 3)


def groups():
    recv, sent = {}, {}
    for c in range(NC + 1):
        for stage in range(S_OWN):
            if c < NC or stage not in (X_FAR, Z_FAR, S_FAR):
                recv[stage, c] = len(set(recv.values()))
        recv[S_OWN, c] = recv[S_NEAR, c]
        if c in (0, NC):
            recv[STATS, c] = len(set(recv.values()))
        for stage in range(STATS + 1):
            if stage in (SHARE, REDUCE):
                sent[stage, c] = 2
            elif c == NC:
                sent[stage, c] = 3 if stage == S_NEAR else 1
            else:
                sent[stage, c] = 0 if stage < SHARE or stage == STATS else 3
    return recv, sent


RECV, SENT = groups()
RECV_COUNT = max(RECV.values()) + 1
WA, OA = sum(IN[:NC]), sum(OUT[:NC])
WB, OB = IN[NC], OUT[NC]
SENT_ALL = (
    (4 * 4 * WA // 128 + 4, 8 * 2 * WB // 128 + 8, 4 * D // 128),
    (3 * 4 * WA // 128 + 3 + 7 * (WA + EXT) // 128,
     7 * 2 * WB // 128 + 7 + 3 * (WB + EXT) // 128 + 3 * OB // 128,
     10 * D // 128,
     (7 * 5 * OA + 15 * 2 * OB) // 128),
)


def pieces(v):
    hi = v.astype(BF16).astype(F32)
    mid = (v - hi).astype(BF16).astype(F32)
    lo = ((v - hi) - mid).astype(BF16).astype(F32)
    return hi, mid, lo


def ext_of(top, mass):
    lane = lax.broadcasted_iota(jnp.int32, (top.shape[0], EXT), 1)
    out = jnp.zeros((top.shape[0], EXT), F32)
    for i, piece in enumerate(pieces(top) + pieces(mass)):
        out = jnp.where(lane == i, piece, out)
    return out


def of_ext(ext):
    e = ext.astype(F32)
    return e[:, 0:1] + e[:, 1:2] + e[:, 2:3], e[:, 3:4] + e[:, 4:5] + e[:, 5:6]


def as_tiles(ext):
    t = ext.T[:16]
    return jnp.stack([t[:, :128], t[:, 128:]]).astype(BF16)


def of_tiles(tiles):
    return tiles.reshape(-1, 128).astype(F32).T


def merge(stats):
    top = stats[0][0]
    for t, _ in stats[1:]:
        top = jnp.maximum(top, t)
    factors = [jnp.exp(t - top) for t, _ in stats]
    mass = factors[0] * stats[0][1]
    for f, (_, m) in zip(factors[1:], stats[1:]):
        mass = mass + f * m
    return factors, top, mass


def pack(v):
    h = v.shape[-1] // 2
    return jnp.concatenate([v[:, :, :h], v[:, :, h:]], axis=1)


def regroup(v):
    return jnp.concatenate(
        [v[(xx * ZN + p) * 8:(xx * ZN + p) * 8 + 8] for p in range(ZN) for xx in range(XN)],
        axis=0,
    )


def weigh(factors, parts):
    total = factors[0] * parts[0].astype(F32)
    for f, p in zip(factors[1:], parts[1:]):
        total = total + f * p.astype(F32)
    return total


def kernel(tok_hbm, sw_hbm, pat_hbm, win_hbm, wout_hbm, mixed, *scratch):
    it = iter(scratch)
    tok, sw, pat, win, wout, turned, wt_ref, probs, table_ref = (next(it) for _ in range(9))
    psend, xbuf, zsend, zbuf = ([next(it) for _ in range(NC)] for _ in range(4))
    ybuf, rsend, rbuf = ([next(it) for _ in range(NC + 1)] for _ in range(3))
    agx = [next(it) for _ in range(NC)]
    qsend, qbuf, rsx, rbx, agz, xstat, xstats, qstat, qstats, yard = (next(it) for _ in range(10))
    load_sem, send_sem, recv_sem = next(it), next(it), next(it)

    seq, clip = lax.axis_index("seq"), lax.axis_index("clip")
    z, x = seq // XN, seq % XN
    y, core = clip // 2, clip % 2

    def dev(dz, dx, dy, k):
        return {
            "seq": ((z + dz) % ZN) * XN + (x + dx) % XN, "clip": ((y + dy) % YN) * 2 + k}

    loads = [
        pltpu.make_async_copy(src, dst, load_sem.at[i])
        for i, (src, dst) in enumerate((
            (sw_hbm, sw), (tok_hbm, tok), (pat_hbm, pat), (win_hbm, win), (wout_hbm, wout)))
    ]
    for load in loads[:3]:
        load.start()

    barrier = pltpu.get_barrier_semaphore()

    def greet(*to):
        pl.semaphore_signal(barrier, inc=1, device_id=dev(*to), device_id_type=MESH)

    for d in XP:
        greet(0, d, 0, 1)
    for d in YP:
        greet(0, 0, d, 1)
    for d in RING[1:]:
        greet(d, 0, 0, 1)

    @pl.when(core == 0)
    def _():
        greet(0, 0, 0, 1)

    @pl.when(core == 1)
    def _():
        greet(0, 0, 0, 0)
        for d in XP:
            greet(0, d, 0, 0)
        for d in YP:
            greet(0, 0, d, 0)
        for d in RING[1:]:
            greet(d, 0, 0, 0)

    def send(stage, c, src, dst, to):
        pltpu.make_async_remote_copy(
            src_ref=src, dst_ref=dst, send_sem=send_sem.at[SENT[stage, c]],
            recv_sem=recv_sem.at[RECV[stage, c]], device_id=dev(*to), device_id_type=MESH,
        ).start()

    def moved(stage, c, view):
        return pltpu.make_async_remote_copy(
            src_ref=view, dst_ref=view, send_sem=send_sem.at[SENT[stage, c]],
            recv_sem=recv_sem.at[RECV[stage, c]], device_id=dev(0, 1, 0, 1),
            device_id_type=MESH,
        )

    def drain(k):
        for i, tiles in enumerate(SENT_ALL[k]):
            view = yard.at[pl.ds(0, tiles)]
            pltpu.make_async_remote_copy(
                src_ref=view, dst_ref=view, send_sem=send_sem.at[i], recv_sem=recv_sem.at[0],
                device_id=dev(0, 1, 0, 1), device_id_type=MESH,
            ).wait_send()

    loads[2].wait()
    group = lax.broadcasted_iota(jnp.int32, (1, SLOTS_ALL), 1) // 4
    named = []
    for b in range(4):
        found = group == pat[b, 0]
        for j in range(1, 16):
            found = jnp.logical_or(found, group == pat[b, j])
        named.append(jnp.where(found, 1.0, 0.0))
    loads[0].wait()
    loads[1].wait()
    loads[3].start()
    loads[4].start()
    logits = []
    for i in range(2):
        rows = slice(i * 256, i * 256 + 256)
        logits.append(jnp.dot(tok[rows], sw[...], preferred_element_type=F32))
        masked = [
            jnp.where(named[2 * i + b] > 0.5, logits[i][b * 128:(b + 1) * 128], LOW)
            for b in range(2)
        ]
        turned[:, rows] = jnp.concatenate(masked, axis=0).T
    logits = jnp.concatenate(logits, axis=0)
    places = [(z + d) % ZN for d in RING]
    rows = jnp.concatenate(
        [turned[pl.ds(pl.multiple_of(zz * 32 + xx * 8, 8), 8), :]
         for xx in range(XN) for zz in places],
        axis=0,
    )
    top = jnp.maximum(jnp.max(rows, axis=1, keepdims=True), EMPTY)
    weights = jnp.exp(rows - top)
    mass = jnp.sum(weights, axis=1, keepdims=True)
    wt_ref[...] = weights.astype(BF16)
    ext = ext_of(top, mass)

    def send_x(stage, c):
        at = 32 if stage == X_FAR else 0
        part = pl.ds(at, 32)

        def rows(d):
            return psend[c].at[pl.ds(pl.multiple_of(((x + d) % XN) * 64 + at, 32), 32)]

        @pl.when(core == 0)
        def _():
            for d in XP + (0,):
                send(stage, c, rows(d), xbuf[c].at[3 + d, part], (0, d, 0, 1))

        @pl.when(core == 1)
        def _():
            for d in XP:
                send(stage, c, rows(d), xbuf[c].at[d - 1, part], (0, d, 0, 1))

    for c in range(NC):
        s, w = IN_AT[c], IN[c]
        part = jnp.dot(wt_ref[...], tok[:, s:s + w], preferred_element_type=F32)
        psend[c][:, 0:w] = part.astype(BF16)
        if c == 0:
            @pl.when(core == 0)
            def _():
                pl.semaphore_wait(barrier, 14)

            @pl.when(core == 1)
            def _():
                pl.semaphore_wait(barrier, 27)

        send_x(X_FAR, c)
        if c == 0:
            send_x(X_NEAR, c)
            xstat[...] = as_tiles(ext)
            qstat[...] = as_tiles(regroup(ext))

            @pl.when(core == 0)
            def _():
                for d in XP + (0,):
                    send(STATS, 0, xstat.at[(x + d) % XN // 2], xstats.at[3 + d], (0, d, 0, 1))
                for p in FAR_FIRST + (0,):
                    send(STATS, NC, qstat.at[p // 4], qstats.at[7 + p], (RING[p], 0, 0, 1))

            @pl.when(core == 1)
            def _():
                for d in XP:
                    send(STATS, 0, xstat.at[(x + d) % XN // 2], xstats.at[d - 1], (0, d, 0, 1))
                for p in FAR_FIRST:
                    send(STATS, NC, qstat.at[p // 4], qstats.at[p - 1], (RING[p], 0, 0, 1))

            part = jnp.dot(wt_ref[...], tok[:, IN_AT[NC]:], preferred_element_type=F32)
            qsend[...] = regroup(part).astype(BF16)

            @pl.when(core == 0)
            def _():
                for p in FAR_FIRST + (0,):
                    send(X_NEAR, NC, qsend.at[pl.ds(32 * p, 32)], qbuf.at[7 + p],
                         (RING[p], 0, 0, 1))

            @pl.when(core == 1)
            def _():
                for p in FAR_FIRST:
                    send(X_NEAR, NC, qsend.at[pl.ds(32 * p, 32)], qbuf.at[p - 1],
                         (RING[p], 0, 0, 1))

    for c in range(1, NC):
        send_x(X_NEAR, c)

    e = jnp.exp(logits - jnp.max(logits, axis=1, keepdims=True))
    probs[...] = (e / jnp.sum(e, axis=1, keepdims=True)).astype(BF16)

    state = {}

    def stage_x(stage, c):
        w = IN[c]
        at = 32 if stage == X_FAR else 0
        half = pl.ds(at // 8, HALF)
        part = slice(at, at + 32)
        mine = pl.ds(pl.multiple_of(x * 64 + at, 32), 32)
        moved(stage, c, xbuf[c].at[:, pl.ds(at, 32)]).wait_recv()

        sources = (
            [xbuf[c][k, part] for k in range(3, 7)],
            [psend[c][mine]] + [xbuf[c][k, part] for k in range(3)],
        )
        if c == 0 and stage == X_FAR:
            moved(STATS, 0, xstats).wait_recv()
            t = of_tiles(jnp.concatenate([xstats[...], xstat[x // 2][None]]))
            t = jnp.where(x % 2 == 0, t[:64], t[64:])
            state["stats"] = [t[:, 16 * k:16 * k + 16] for k in (3, 4, 5, 6, 7, 0, 1, 2)]
        if c == 0:
            stats = [of_ext(t[part]) for t in state["stats"]]
            state[stage] = [merge(stats[:4]), merge(stats[4:])]
            exts = [ext_of(t, m).reshape(HALF, 8, EXT) for _, t, m in state[stage]]
            zsend[0][half, :, w:] = jnp.concatenate(exts, axis=1).astype(BF16)
        totals = [
            weigh(factors, parts).reshape(HALF, 8, w)
            for (factors, _, _), parts in zip(state[stage], sources)
        ]
        zsend[c][half, :, 0:w] = jnp.concatenate(totals, axis=1).astype(BF16)
        for p in FAR_FIRST:
            if (p >= HALF) == (stage == X_FAR):
                send(Z_IN, c, zsend[c].at[p], zbuf[c].at[p - 1], (RING[p], 0, 0, 1))

    def stage_z(c):
        w = IN[c]
        moved(Z_IN, c, zbuf[c]).wait_recv()
        if c == 0:
            exts = [zsend[0][0, :, w:]] + [zbuf[0][k, :, w:] for k in range(7)]
            factors, _, mass = merge([of_ext(e) for e in exts])
            state["z"] = [f / mass for f in factors]
        parts = [zsend[c][0, :, 0:w]] + [zbuf[c][k, :, 0:w] for k in range(7)]
        share(c, weigh(state["z"], parts))

    def stage_qstats():
        moved(STATS, NC, qstats).wait_recv()
        t = of_tiles(jnp.concatenate([qstats[...], qstat[0:1]]))
        stats = [
            of_ext(t[32 * (p % 4):32 * (p % 4) + 32, 16 * k:16 * k + 16])
            for p, k in [(p, 7 + p) for p in range(8)] + [(0, 15)] + [(p, p - 1) for p in range(1, 8)]
        ]
        state["q"] = [merge(stats[:8]), merge(stats[8:])]
        merged = [ext_of(top, mass).reshape(XN, 8, EXT) for _, top, mass in state["q"]]
        rsx[:, :, IN[NC]:] = jnp.concatenate(merged, axis=1).astype(BF16)

    def stage_qz():
        w = IN[NC]
        moved(X_NEAR, NC, qbuf).wait_recv()
        sources = (
            [qbuf[k] for k in range(7, 15)],
            [qsend[0:32, :]] + [qbuf[k] for k in range(7)],
        )
        totals = [
            weigh(factors, parts).reshape(XN, 8, w)
            for (factors, _, _), parts in zip(state["q"], sources)
        ]
        rsx[:, :, 0:w] = jnp.concatenate(totals, axis=1).astype(BF16)
        for d in XP:
            send(Z_IN, NC, rsx.at[(x + d) % XN], rbx.at[d - 1], (0, d, 0, 1))

    def stage_qx():
        w = IN[NC]
        moved(Z_IN, NC, rbx).wait_recv()
        parts = [rsx[x]] + [rbx[k] for k in range(3)]
        factors, _, mass = merge([of_ext(p[:, w:]) for p in parts])
        share(NC, weigh([f / mass for f in factors], [p[:, 0:w] for p in parts]))

    def share(c, total):
        ybuf[c][0] = total.astype(BF16)
        for d in YP:
            send(SHARE, c, ybuf[c].at[0], ybuf[c].at[d], (0, 0, d, 0))
        send(SHARE, c, ybuf[c].at[0], ybuf[c].at[0], (0, 0, 0, 0))
        for d in YP:
            send(SHARE, c, ybuf[c].at[0], ybuf[c].at[d], (0, 0, d, 1))

    def stage_in(c):
        s, w = IN_AT[c], IN[c]

        @pl.when(core == 0)
        def _():
            moved(SHARE, c, ybuf[c]).wait_recv()

        @pl.when(core == 1)
        def _():
            moved(SHARE, c, ybuf[c].at[pl.ds(1, 3)]).wait_recv()

        if c == 0:
            loads[3].wait()
        rows = ybuf[c][...].reshape(64, w)
        inner = [jnp.dot(rows, win[e, s:s + w, :], preferred_element_type=F32) for e in range(2)]
        if c == 0:
            state["inner"] = inner
        else:
            state["inner"] = [a + b for a, b in zip(state["inner"], inner)]

    def stage_out(c):
        s, w = OUT_AT[c], OUT[c]
        if c == 0:
            loads[4].wait()
            first = lax.broadcasted_iota(jnp.int32, (64, FS), 0) % 8 < 4
            act = jax.nn.gelu(jnp.where(first, *state["inner"]), approximate=True)
            state["active"] = jnp.concatenate(
                [jnp.where(first, act, 0.0), jnp.where(first, 0.0, act)], axis=1).astype(BF16)
        if c < 2:
            lanes = slice(0, OUT[0]) if c == 0 else slice(OUT[0], D)
            state["outer"] = jnp.dot(
                state["active"], wout[:, lanes], preferred_element_type=F32)
            state["at"] = lanes.start
        outer = state["outer"][:, s - state["at"]:s - state["at"] + w]
        rsend[c][...] = outer.reshape(YN, 16, w).astype(BF16)

        @pl.when(core == 0)
        def _():
            for d in YP + (0,):
                send(REDUCE, c, rsend[c].at[d], rbuf[c].at[3 + d], (0, 0, YN - d, 1))

        @pl.when(core == 1)
        def _():
            for d in YP:
                send(REDUCE, c, rsend[c].at[d], rbuf[c].at[d - 1], (0, 0, YN - d, 1))

    def stage_sum(c):
        w = OUT[c]
        moved(REDUCE, c, rbuf[c]).wait_recv()
        total = rsend[c][0].astype(F32)
        for k in range(7):
            total = total + rbuf[c][k].astype(F32)
        total = pack(total.reshape(2, 8, w)).astype(BF16)
        if c == NC:
            agz[z, x] = total
            for d in XP:
                send(Z_NEAR, NC, agz.at[z, x], agz.at[z, x], (0, d, 0, 1))
        else:
            agx[c][x, 0] = total
            for p in range(1, NEAR):
                send(Z_NEAR, c, agx[c].at[x, 0], agx[c].at[x, p], (ZN - RING[p], 0, 0, 1))
            spread(S_OWN, c)
            for p in range(NEAR, ZN):
                send(Z_FAR, c, agx[c].at[x, 0], agx[c].at[x, p], (ZN - RING[p], 0, 0, 1))

    def stage_spread_z():
        moved(Z_NEAR, NC, agz.at[0, pl.ds(0, 3)]).wait_recv()
        for p in FAR_FIRST:
            send(S_NEAR, NC, agz.at[z, :, 0], agz.at[z, :, 0], (RING[p], 0, 0, 0))
            send(S_NEAR, NC, agz.at[z, :, 1], agz.at[z, :, 1], (RING[p], 0, 0, 1))
        send(S_NEAR, NC, agz.at[z, :, 0], agz.at[z, :, 0], (0, 0, 0, 0))

    def stage_near(c):
        moved(Z_NEAR, c, agx[c].at[0, pl.ds(1, NEAR - 1)]).wait_recv()
        spread(S_NEAR, c)

    def stage_far(c):
        moved(Z_FAR, c, agx[c].at[0, pl.ds(NEAR, ZN - NEAR)]).wait_recv()
        spread(S_FAR, c)

    def spread(stage, c):
        places = pl.ds(*PARTS[stage])
        for d in XP:
            part = agx[c].at[x, places, 0]
            send(stage, c, part, part, (0, d, 0, 0))
            part = agx[c].at[x, places, 1]
            send(stage, c, part, part, (0, d, 0, 1))
        part = agx[c].at[x, places, 0]
        send(stage, c, part, part, (0, 0, 0, 0))

    def stage_mix_z():
        @pl.when(core == 0)
        def _():
            moved(S_NEAR, NC, agz.at[:, :, 0]).wait_recv()

        @pl.when(core == 1)
        def _():
            moved(S_NEAR, NC, agz.at[pl.ds(0, 7), :, 0]).wait_recv()

        rows = agz[:, :, core].astype(F32).reshape(ZN * XN, 16, OUT[NC] // 2)
        table_ref[:, OUT_AT[NC]:] = jnp.concatenate(
            [rows[:, :8], rows[:, 8:]], axis=2).reshape(SLOTS_ALL, OUT[NC]).astype(BF16)

    def stage_mix(stage, c):
        s, w = OUT_AT[c], OUT[c]
        first, count = PARTS[stage]
        if stage == S_NEAR:
            first, count = 0, NEAR

        @pl.when(core == 0)
        def _():
            moved(stage, c, agx[c].at[:, pl.ds(first, count), 0]).wait_recv()

        @pl.when(core == 1)
        def _():
            moved(stage, c, agx[c].at[pl.ds(0, 3), pl.ds(first, count), 0]).wait_recv()

        for p in range(first, first + count):
            rows = agx[c][:, p, core].astype(F32)
            at = pl.ds(pl.multiple_of(places[p] * 32, 32), 32)
            table_ref[at, s:s + w] = jnp.concatenate(
                [rows[:, :8], rows[:, 8:]], axis=2).reshape(32, w).astype(BF16)

    @pl.when(core == 1)
    def _():
        stage_x(X_FAR, 0)
        stage_x(X_NEAR, 0)
        stage_x(X_FAR, 1)
        stage_x(X_FAR, 2)
        stage_qstats()
        stage_x(X_NEAR, 1)
        stage_x(X_NEAR, 2)
        stage_qz()
        stage_z(0)
        stage_z(1)
        stage_qx()
        stage_z(2)

    for c in ORDER:
        stage_in(c)
    for c in ORDER:
        stage_out(c)

    @pl.when(core == 1)
    def _():
        for c in ORDER:
            stage_sum(c)
        stage_near(0)
        stage_near(1)
        stage_spread_z()
        stage_far(0)
        stage_near(2)
        stage_far(1)
        stage_far(2)

    stage_mix(S_NEAR, 0)
    stage_mix(S_NEAR, 1)

    def finish(c):
        lanes = slice(OUT_AT[c], OUT_AT[c] + OUT[c])
        mixed[:, lanes] = jnp.dot(
            probs[...], table_ref[:, lanes], preferred_element_type=F32).astype(BF16)

    stage_mix(S_FAR, 0)
    finish(0)
    stage_mix_z()
    finish(NC)
    stage_mix(S_NEAR, 2)
    stage_mix(S_FAR, 1)
    finish(1)
    stage_mix(S_FAR, 2)
    finish(2)

    @pl.when(core == 0)
    def _():
        drain(0)

    @pl.when(core == 1)
    def _():
        drain(1)


def local(tokens, slot_weight, pattern, w_in, w_out):
    def vm(*shape):
        return pltpu.VMEM(shape, BF16)

    first = [w + (EXT if c == 0 else 0) for c, w in enumerate(IN[:NC])]
    scratch = [
        vm(TOK, D), vm(D, SLOTS_ALL), pltpu.SMEM((4, 16), jnp.int32),
        vm(2, D, FS), vm(2 * FS, D), pltpu.VMEM((SLOTS_ALL, TOK), F32), vm(SLOTS_ALL, TOK),
        vm(TOK, SLOTS_ALL), vm(SLOTS_ALL, D)]
    scratch += [vm(SLOTS_ALL, w) for w in IN[:NC]]
    scratch += [vm(7, 64, w) for w in IN[:NC]]
    scratch += [vm(ZN, 16, w) for w in first]
    scratch += [vm(7, 16, w) for w in first]
    scratch += [vm(YN, 16, w) for w in IN]
    scratch += [vm(YN, 16, w) for w in OUT]
    scratch += [vm(7, 16, w) for w in OUT]
    scratch += [vm(XN, ZN, 2, 16, w // 2) for w in OUT[:NC]]
    last = IN[NC] + EXT
    scratch += [
        vm(SLOTS_ALL, IN[NC]), vm(15, 32, IN[NC]), vm(XN, 16, last), vm(3, 16, last),
        vm(ZN, XN, 2, 16, OUT[NC] // 2),
        vm(2, 16, 128), vm(7, 16, 128), vm(2, 16, 128), vm(15, 16, 128),
        vm(max(max(tiles) for tiles in SENT_ALL), 16, 128),
        pltpu.SemaphoreType.DMA((5,)),
        pltpu.SemaphoreType.DMA((4,)), pltpu.SemaphoreType.DMA((RECV_COUNT,)),
    ]
    arrays = (tokens.reshape(TOK, D), slot_weight, pattern, w_in, w_out.reshape(2 * FS, D))
    hbm = pl.BlockSpec(memory_space=pltpu.HBM)
    vmem = pl.BlockSpec(memory_space=pltpu.VMEM)
    mixed = pl.pallas_call(
        kernel,
        out_shape=pltpu.VMEM((TOK, D), BF16),
        in_specs=[hbm, hbm, hbm, hbm, hbm],
        out_specs=vmem,
        scratch_shapes=scratch,
        compiler_params=pltpu.CompilerParams(
            collective_id=0, has_side_effects=True, vmem_limit_bytes=40 << 20),
        name="layer",
    )(*(pltpu.with_memory_space_constraint(a, pltpu.HBM) for a in arrays))
    return mixed.reshape(tokens.shape)


def solution(mesh):
    in_specs = (
        P("clip", "seq", None),
        P(),
        P("seq", None),
        P("seq", None, "clip"),
        P("seq", "clip", None),
    )
    return jax.shard_map(
        local, mesh=mesh, in_specs=in_specs, out_specs=P("clip", "seq", None), check_vma=False)
```

```python
import jax
import jax.numpy as jnp
from jax import lax
from jax.experimental import pallas as pl
from jax.experimental.pallas import tpu as pltpu
from jax.sharding import PartitionSpec as P

MESH = pl.DeviceIdType.MESH
BF16, F32 = jnp.bfloat16, jnp.float32
D = 1280
FS = 640
TOK = 512
SLOTS_ALL = 256
ZN, XN, YN = 8, 4, 4
EXT = 128
IN = (256, 512, 256, 256)
IN_AT = tuple(sum(IN[:i]) for i in range(len(IN)))
OUT = (256, 256, 512, 256)
OUT_AT = tuple(sum(OUT[:i]) for i in range(len(OUT)))
NC = 3
ORDER = (0, 1, NC, 2)
RING = (0, 1, 7, 2, 6, 3, 5, 4)
FAR_FIRST = (7, 5, 6, 4, 3, 1, 2)
HALF = 4
NEAR = 5
(X_NEAR, X_FAR, Z_IN, SHARE, REDUCE, Z_NEAR, Z_FAR, S_NEAR, S_FAR, S_OWN, STATS) = range(11)
PARTS = {S_OWN: (0, 1), S_NEAR: (1, NEAR - 1), S_FAR: (NEAR, ZN - NEAR)}
LOW = -1.0e30
EMPTY = -1.0e29

XP = (2, 1, 3)
ZP = (4, 3, 5, 2, 6, 1, 7)
YP = (2, 1, 3)


def groups():
    recv, sent = {}, {}
    for c in range(NC + 1):
        for stage in range(S_OWN):
            if c < NC or stage not in (X_FAR, Z_FAR, S_FAR):
                recv[stage, c] = len(set(recv.values()))
        recv[S_OWN, c] = recv[S_NEAR, c]
        if c in (0, NC):
            recv[STATS, c] = len(set(recv.values()))
        for stage in range(STATS + 1):
            if stage in (SHARE, REDUCE):
                sent[stage, c] = 2
            elif c == NC:
                sent[stage, c] = 3 if stage == S_NEAR else 1
            else:
                sent[stage, c] = 0 if stage < SHARE or stage == STATS else 3
    return recv, sent


RECV, SENT = groups()
RECV_COUNT = max(RECV.values()) + 1
WA, OA = sum(IN[:NC]), sum(OUT[:NC])
WB, OB = IN[NC], OUT[NC]
SENT_ALL = (
    (4 * 4 * WA // 128 + 4, 8 * 2 * WB // 128 + 8, 4 * D // 128),
    (3 * 4 * WA // 128 + 3 + 7 * (WA + EXT) // 128,
     7 * 2 * WB // 128 + 7 + 3 * (WB + EXT) // 128 + 3 * OB // 128,
     10 * D // 128,
     (7 * 5 * OA + 15 * 2 * OB) // 128),
)


def pieces(v):
    hi = v.astype(BF16).astype(F32)
    mid = (v - hi).astype(BF16).astype(F32)
    lo = ((v - hi) - mid).astype(BF16).astype(F32)
    return hi, mid, lo


def ext_of(top, mass):
    lane = lax.broadcasted_iota(jnp.int32, (top.shape[0], EXT), 1)
    out = jnp.zeros((top.shape[0], EXT), F32)
    for i, piece in enumerate(pieces(top) + pieces(mass)):
        out = jnp.where(lane == i, piece, out)
    return out


def of_ext(ext):
    e = ext.astype(F32)
    return e[:, 0:1] + e[:, 1:2] + e[:, 2:3], e[:, 3:4] + e[:, 4:5] + e[:, 5:6]


def as_tiles(ext):
    t = ext.T[:16]
    return jnp.stack([t[:, :128], t[:, 128:]]).astype(BF16)


def of_tiles(tiles):
    return tiles.reshape(-1, 128).astype(F32).T


def merge(stats):
    top = stats[0][0]
    for t, _ in stats[1:]:
        top = jnp.maximum(top, t)
    factors = [jnp.exp(t - top) for t, _ in stats]
    mass = factors[0] * stats[0][1]
    for f, (_, m) in zip(factors[1:], stats[1:]):
        mass = mass + f * m
    return factors, top, mass


def pack(v):
    h = v.shape[-1] // 2
    return jnp.concatenate([v[:, :, :h], v[:, :, h:]], axis=1)


def regroup(v):
    return jnp.concatenate(
        [v[(xx * ZN + p) * 8:(xx * ZN + p) * 8 + 8] for p in range(ZN) for xx in range(XN)],
        axis=0,
    )


def weigh(factors, parts):
    total = factors[0] * parts[0].astype(F32)
    for f, p in zip(factors[1:], parts[1:]):
        total = total + f * p.astype(F32)
    return total


def kernel(tok_hbm, sw_hbm, pat_hbm, win_hbm, wout_hbm, mixed, *scratch):
    it = iter(scratch)
    tok, sw, pat, win, wout, turned, wt_ref, probs, table_ref = (next(it) for _ in range(9))
    psend, xbuf, zsend, zbuf = ([next(it) for _ in range(NC)] for _ in range(4))
    ybuf, rsend, rbuf = ([next(it) for _ in range(NC + 1)] for _ in range(3))
    agx = [next(it) for _ in range(NC)]
    qsend, qbuf, rsx, rbx, agz, xstat, xstats, qstat, qstats, yard = (next(it) for _ in range(10))
    load_sem, send_sem, recv_sem = next(it), next(it), next(it)

    seq, clip = lax.axis_index("seq"), lax.axis_index("clip")
    z, x = seq // XN, seq % XN
    y, core = clip // 2, clip % 2

    def dev(dz, dx, dy, k):
        return {
            "seq": ((z + dz) % ZN) * XN + (x + dx) % XN, "clip": ((y + dy) % YN) * 2 + k}

    loads = [
        pltpu.make_async_copy(src, dst, load_sem.at[i])
        for i, (src, dst) in enumerate((
            (sw_hbm, sw), (tok_hbm, tok), (pat_hbm, pat), (win_hbm, win), (wout_hbm, wout)))
    ]
    for load in loads[:3]:
        load.start()

    barrier = pltpu.get_barrier_semaphore()

    def greet(*to):
        pl.semaphore_signal(barrier, inc=1, device_id=dev(*to), device_id_type=MESH)

    for d in XP:
        greet(0, d, 0, 1)
    for d in YP:
        greet(0, 0, d, 1)
    for d in RING[1:]:
        greet(d, 0, 0, 1)

    @pl.when(core == 0)
    def _():
        greet(0, 0, 0, 1)

    @pl.when(core == 1)
    def _():
        greet(0, 0, 0, 0)
        for d in XP:
            greet(0, d, 0, 0)
        for d in YP:
            greet(0, 0, d, 0)
        for d in RING[1:]:
            greet(d, 0, 0, 0)

    def send(stage, c, src, dst, to):
        pltpu.make_async_remote_copy(
            src_ref=src, dst_ref=dst, send_sem=send_sem.at[SENT[stage, c]],
            recv_sem=recv_sem.at[RECV[stage, c]], device_id=dev(*to), device_id_type=MESH,
        ).start()

    def moved(stage, c, view):
        return pltpu.make_async_remote_copy(
            src_ref=view, dst_ref=view, send_sem=send_sem.at[SENT[stage, c]],
            recv_sem=recv_sem.at[RECV[stage, c]], device_id=dev(0, 1, 0, 1),
            device_id_type=MESH,
        )

    def drain(k):
        for i, tiles in enumerate(SENT_ALL[k]):
            view = yard.at[pl.ds(0, tiles)]
            pltpu.make_async_remote_copy(
                src_ref=view, dst_ref=view, send_sem=send_sem.at[i], recv_sem=recv_sem.at[0],
                device_id=dev(0, 1, 0, 1), device_id_type=MESH,
            ).wait_send()

    loads[2].wait()
    group = lax.broadcasted_iota(jnp.int32, (1, SLOTS_ALL), 1) // 4
    named = []
    for b in range(4):
        found = group == pat[b, 0]
        for j in range(1, 16):
            found = jnp.logical_or(found, group == pat[b, j])
        named.append(jnp.where(found, 1.0, 0.0))
    loads[0].wait()
    loads[1].wait()
    loads[3].start()
    loads[4].start()
    logits = []
    for i in range(2):
        rows = slice(i * 256, i * 256 + 256)
        logits.append(jnp.dot(tok[rows], sw[...], preferred_element_type=F32))
        masked = [
            jnp.where(named[2 * i + b] > 0.5, logits[i][b * 128:(b + 1) * 128], LOW)
            for b in range(2)
        ]
        turned[:, rows] = jnp.concatenate(masked, axis=0).T
    logits = jnp.concatenate(logits, axis=0)
    places = [(z + d) % ZN for d in RING]
    rows = jnp.concatenate(
        [turned[pl.ds(pl.multiple_of(zz * 32 + xx * 8, 8), 8), :]
         for xx in range(XN) for zz in places],
        axis=0,
    )
    top = jnp.maximum(jnp.max(rows, axis=1, keepdims=True), EMPTY)
    weights = jnp.exp(rows - top)
    mass = jnp.sum(weights, axis=1, keepdims=True)
    wt_ref[...] = weights.astype(BF16)
    ext = ext_of(top, mass)

    def send_x(stage, c):
        at = 32 if stage == X_FAR else 0
        part = pl.ds(at, 32)

        def rows(d):
            return psend[c].at[pl.ds(pl.multiple_of(((x + d) % XN) * 64 + at, 32), 32)]

        @pl.when(core == 0)
        def _():
            for d in XP + (0,):
                send(stage, c, rows(d), xbuf[c].at[3 + d, part], (0, d, 0, 1))

        @pl.when(core == 1)
        def _():
            for d in XP:
                send(stage, c, rows(d), xbuf[c].at[d - 1, part], (0, d, 0, 1))

    for c in range(NC):
        s, w = IN_AT[c], IN[c]
        part = jnp.dot(wt_ref[...], tok[:, s:s + w], preferred_element_type=F32)
        psend[c][:, 0:w] = part.astype(BF16)
        if c == 0:
            @pl.when(core == 0)
            def _():
                pl.semaphore_wait(barrier, 14)

            @pl.when(core == 1)
            def _():
                pl.semaphore_wait(barrier, 27)

        send_x(X_FAR, c)
        if c == 0:
            send_x(X_NEAR, c)
            xstat[...] = as_tiles(ext)
            qstat[...] = as_tiles(regroup(ext))

            @pl.when(core == 0)
            def _():
                for d in XP + (0,):
                    send(STATS, 0, xstat.at[(x + d) % XN // 2], xstats.at[3 + d], (0, d, 0, 1))
                for p in FAR_FIRST + (0,):
                    send(STATS, NC, qstat.at[p // 4], qstats.at[7 + p], (RING[p], 0, 0, 1))

            @pl.when(core == 1)
            def _():
                for d in XP:
                    send(STATS, 0, xstat.at[(x + d) % XN // 2], xstats.at[d - 1], (0, d, 0, 1))
                for p in FAR_FIRST:
                    send(STATS, NC, qstat.at[p // 4], qstats.at[p - 1], (RING[p], 0, 0, 1))

            part = jnp.dot(wt_ref[...], tok[:, IN_AT[NC]:], preferred_element_type=F32)
            qsend[...] = regroup(part).astype(BF16)

            @pl.when(core == 0)
            def _():
                for p in FAR_FIRST + (0,):
                    send(X_NEAR, NC, qsend.at[pl.ds(32 * p, 32)], qbuf.at[7 + p],
                         (RING[p], 0, 0, 1))

            @pl.when(core == 1)
            def _():
                for p in FAR_FIRST:
                    send(X_NEAR, NC, qsend.at[pl.ds(32 * p, 32)], qbuf.at[p - 1],
                         (RING[p], 0, 0, 1))

    for c in range(1, NC):
        send_x(X_NEAR, c)

    e = jnp.exp(logits - jnp.max(logits, axis=1, keepdims=True))
    probs[...] = (e / jnp.sum(e, axis=1, keepdims=True)).astype(BF16)

    state = {}

    def stage_x(stage, c):
        w = IN[c]
        at = 32 if stage == X_FAR else 0
        half = pl.ds(at // 8, HALF)
        part = slice(at, at + 32)
        mine = pl.ds(pl.multiple_of(x * 64 + at, 32), 32)
        moved(stage, c, xbuf[c].at[:, pl.ds(at, 32)]).wait_recv()

        sources = (
            [xbuf[c][k, part] for k in range(3, 7)],
            [psend[c][mine]] + [xbuf[c][k, part] for k in range(3)],
        )
        if c == 0 and stage == X_FAR:
            moved(STATS, 0, xstats).wait_recv()
            t = of_tiles(jnp.concatenate([xstats[...], xstat[x // 2][None]]))
            t = jnp.where(x % 2 == 0, t[:64], t[64:])
            state["stats"] = [t[:, 16 * k:16 * k + 16] for k in (3, 4, 5, 6, 7, 0, 1, 2)]
        if c == 0:
            stats = [of_ext(t[part]) for t in state["stats"]]
            state[stage] = [merge(stats[:4]), merge(stats[4:])]
            exts = [ext_of(t, m).reshape(HALF, 8, EXT) for _, t, m in state[stage]]
            zsend[0][half, :, w:] = jnp.concatenate(exts, axis=1).astype(BF16)
        totals = [
            weigh(factors, parts).reshape(HALF, 8, w)
            for (factors, _, _), parts in zip(state[stage], sources)
        ]
        zsend[c][half, :, 0:w] = jnp.concatenate(totals, axis=1).astype(BF16)
        for p in FAR_FIRST:
            if (p >= HALF) == (stage == X_FAR):
                send(Z_IN, c, zsend[c].at[p], zbuf[c].at[p - 1], (RING[p], 0, 0, 1))

    def stage_z(c):
        w = IN[c]
        moved(Z_IN, c, zbuf[c]).wait_recv()
        if c == 0:
            exts = [zsend[0][0, :, w:]] + [zbuf[0][k, :, w:] for k in range(7)]
            factors, _, mass = merge([of_ext(e) for e in exts])
            state["z"] = [f / mass for f in factors]
        parts = [zsend[c][0, :, 0:w]] + [zbuf[c][k, :, 0:w] for k in range(7)]
        share(c, weigh(state["z"], parts))

    def stage_qstats():
        moved(STATS, NC, qstats).wait_recv()
        t = of_tiles(jnp.concatenate([qstats[...], qstat[0:1]]))
        stats = [
            of_ext(t[32 * (p % 4):32 * (p % 4) + 32, 16 * k:16 * k + 16])
            for p, k in [(p, 7 + p) for p in range(8)] + [(0, 15)] + [(p, p - 1) for p in range(1, 8)]
        ]
        state["q"] = [merge(stats[:8]), merge(stats[8:])]
        merged = [ext_of(top, mass).reshape(XN, 8, EXT) for _, top, mass in state["q"]]
        rsx[:, :, IN[NC]:] = jnp.concatenate(merged, axis=1).astype(BF16)

    def stage_qz():
        w = IN[NC]
        moved(X_NEAR, NC, qbuf).wait_recv()
        sources = (
            [qbuf[k] for k in range(7, 15)],
            [qsend[0:32, :]] + [qbuf[k] for k in range(7)],
        )
        totals = [
            weigh(factors, parts).reshape(XN, 8, w)
            for (factors, _, _), parts in zip(state["q"], sources)
        ]
        rsx[:, :, 0:w] = jnp.concatenate(totals, axis=1).astype(BF16)
        for d in XP:
            send(Z_IN, NC, rsx.at[(x + d) % XN], rbx.at[d - 1], (0, d, 0, 1))

    def stage_qx():
        w = IN[NC]
        moved(Z_IN, NC, rbx).wait_recv()
        parts = [rsx[x]] + [rbx[k] for k in range(3)]
        factors, _, mass = merge([of_ext(p[:, w:]) for p in parts])
        share(NC, weigh([f / mass for f in factors], [p[:, 0:w] for p in parts]))

    def share(c, total):
        ybuf[c][0] = total.astype(BF16)
        for d in YP:
            send(SHARE, c, ybuf[c].at[0], ybuf[c].at[d], (0, 0, d, 0))
        send(SHARE, c, ybuf[c].at[0], ybuf[c].at[0], (0, 0, 0, 0))
        for d in YP:
            send(SHARE, c, ybuf[c].at[0], ybuf[c].at[d], (0, 0, d, 1))

    def stage_in(c):
        s, w = IN_AT[c], IN[c]

        @pl.when(core == 0)
        def _():
            moved(SHARE, c, ybuf[c]).wait_recv()

        @pl.when(core == 1)
        def _():
            moved(SHARE, c, ybuf[c].at[pl.ds(1, 3)]).wait_recv()

        if c == 0:
            loads[3].wait()
        rows = ybuf[c][...].reshape(64, w)
        inner = [jnp.dot(rows, win[e, s:s + w, :], preferred_element_type=F32) for e in range(2)]
        if c == 0:
            state["inner"] = inner
        else:
            state["inner"] = [a + b for a, b in zip(state["inner"], inner)]

    def stage_out(c):
        s, w = OUT_AT[c], OUT[c]
        if c == 0:
            loads[4].wait()
            first = lax.broadcasted_iota(jnp.int32, (64, FS), 0) % 8 < 4
            act = jax.nn.gelu(jnp.where(first, *state["inner"]), approximate=True)
            state["active"] = jnp.concatenate(
                [jnp.where(first, act, 0.0), jnp.where(first, 0.0, act)], axis=1).astype(BF16)
        if c < 2:
            lanes = slice(0, OUT[0]) if c == 0 else slice(OUT[0], D)
            state["outer"] = jnp.dot(
                state["active"], wout[:, lanes], preferred_element_type=F32)
            state["at"] = lanes.start
        outer = state["outer"][:, s - state["at"]:s - state["at"] + w]
        rsend[c][...] = outer.reshape(YN, 16, w).astype(BF16)

        @pl.when(core == 0)
        def _():
            for d in YP + (0,):
                send(REDUCE, c, rsend[c].at[d], rbuf[c].at[3 + d], (0, 0, YN - d, 1))

        @pl.when(core == 1)
        def _():
            for d in YP:
                send(REDUCE, c, rsend[c].at[d], rbuf[c].at[d - 1], (0, 0, YN - d, 1))

    def stage_sum(c):
        w = OUT[c]
        moved(REDUCE, c, rbuf[c]).wait_recv()
        total = rsend[c][0].astype(F32)
        for k in range(7):
            total = total + rbuf[c][k].astype(F32)
        total = pack(total.reshape(2, 8, w)).astype(BF16)
        if c == NC:
            agz[z, x] = total
            for d in XP:
                send(Z_NEAR, NC, agz.at[z, x], agz.at[z, x], (0, d, 0, 1))
        else:
            agx[c][x, 0] = total
            for p in range(1, NEAR):
                send(Z_NEAR, c, agx[c].at[x, 0], agx[c].at[x, p], (ZN - RING[p], 0, 0, 1))
            for p in range(ZN - 1, NEAR - 1, -1):
                send(Z_FAR, c, agx[c].at[x, 0], agx[c].at[x, p], (ZN - RING[p], 0, 0, 1))
            spread(S_OWN, c)

    def stage_spread_z():
        moved(Z_NEAR, NC, agz.at[0, pl.ds(0, 3)]).wait_recv()
        for p in FAR_FIRST:
            send(S_NEAR, NC, agz.at[z, :, 0], agz.at[z, :, 0], (RING[p], 0, 0, 0))
            send(S_NEAR, NC, agz.at[z, :, 1], agz.at[z, :, 1], (RING[p], 0, 0, 1))
        send(S_NEAR, NC, agz.at[z, :, 0], agz.at[z, :, 0], (0, 0, 0, 0))

    def stage_near(c):
        moved(Z_NEAR, c, agx[c].at[0, pl.ds(1, NEAR - 1)]).wait_recv()
        spread(S_NEAR, c)

    def stage_far(c):
        moved(Z_FAR, c, agx[c].at[0, pl.ds(NEAR, ZN - NEAR)]).wait_recv()
        spread(S_FAR, c)

    def spread(stage, c):
        places = pl.ds(*PARTS[stage])
        for d in XP:
            part = agx[c].at[x, places, 0]
            send(stage, c, part, part, (0, d, 0, 0))
            part = agx[c].at[x, places, 1]
            send(stage, c, part, part, (0, d, 0, 1))
        part = agx[c].at[x, places, 0]
        send(stage, c, part, part, (0, 0, 0, 0))

    def stage_mix_z():
        @pl.when(core == 0)
        def _():
            moved(S_NEAR, NC, agz.at[:, :, 0]).wait_recv()

        @pl.when(core == 1)
        def _():
            moved(S_NEAR, NC, agz.at[pl.ds(0, 7), :, 0]).wait_recv()

        rows = agz[:, :, core].astype(F32).reshape(ZN * XN, 16, OUT[NC] // 2)
        table_ref[:, OUT_AT[NC]:] = jnp.concatenate(
            [rows[:, :8], rows[:, 8:]], axis=2).reshape(SLOTS_ALL, OUT[NC]).astype(BF16)

    def stage_mix(stage, c):
        s, w = OUT_AT[c], OUT[c]
        first, count = PARTS[stage]
        if stage == S_NEAR:
            first, count = 0, NEAR

        @pl.when(core == 0)
        def _():
            moved(stage, c, agx[c].at[:, pl.ds(first, count), 0]).wait_recv()

        @pl.when(core == 1)
        def _():
            moved(stage, c, agx[c].at[pl.ds(0, 3), pl.ds(first, count), 0]).wait_recv()

        for p in range(first, first + count):
            rows = agx[c][:, p, core].astype(F32)
            at = pl.ds(pl.multiple_of(places[p] * 32, 32), 32)
            table_ref[at, s:s + w] = jnp.concatenate(
                [rows[:, :8], rows[:, 8:]], axis=2).reshape(32, w).astype(BF16)

    @pl.when(core == 1)
    def _():
        stage_x(X_FAR, 0)
        stage_x(X_NEAR, 0)
        stage_x(X_FAR, 1)
        stage_x(X_FAR, 2)
        stage_qstats()
        stage_x(X_NEAR, 1)
        stage_x(X_NEAR, 2)
        stage_qz()
        stage_z(0)
        stage_z(1)
        stage_qx()
        stage_z(2)

    for c in ORDER:
        stage_in(c)
    for c in ORDER:
        stage_out(c)

    @pl.when(core == 1)
    def _():
        for c in ORDER:
            stage_sum(c)
        stage_near(0)
        stage_near(1)
        stage_spread_z()
        stage_far(0)
        stage_near(2)
        stage_far(1)
        stage_far(2)

    stage_mix(S_NEAR, 0)
    stage_mix(S_NEAR, 1)

    def finish(c):
        lanes = slice(OUT_AT[c], OUT_AT[c] + OUT[c])
        mixed[:, lanes] = jnp.dot(
            probs[...], table_ref[:, lanes], preferred_element_type=F32).astype(BF16)

    stage_mix(S_FAR, 0)
    finish(0)
    stage_mix_z()
    finish(NC)
    stage_mix(S_NEAR, 2)
    stage_mix(S_FAR, 1)
    finish(1)
    stage_mix(S_FAR, 2)
    finish(2)

    @pl.when(core == 0)
    def _():
        drain(0)

    @pl.when(core == 1)
    def _():
        drain(1)


def local(tokens, slot_weight, pattern, w_in, w_out):
    def vm(*shape):
        return pltpu.VMEM(shape, BF16)

    first = [w + (EXT if c == 0 else 0) for c, w in enumerate(IN[:NC])]
    scratch = [
        vm(TOK, D), vm(D, SLOTS_ALL), pltpu.SMEM((4, 16), jnp.int32),
        vm(2, D, FS), vm(2 * FS, D), pltpu.VMEM((SLOTS_ALL, TOK), F32), vm(SLOTS_ALL, TOK),
        vm(TOK, SLOTS_ALL), vm(SLOTS_ALL, D)]
    scratch += [vm(SLOTS_ALL, w) for w in IN[:NC]]
    scratch += [vm(7, 64, w) for w in IN[:NC]]
    scratch += [vm(ZN, 16, w) for w in first]
    scratch += [vm(7, 16, w) for w in first]
    scratch += [vm(YN, 16, w) for w in IN]
    scratch += [vm(YN, 16, w) for w in OUT]
    scratch += [vm(7, 16, w) for w in OUT]
    scratch += [vm(XN, ZN, 2, 16, w // 2) for w in OUT[:NC]]
    last = IN[NC] + EXT
    scratch += [
        vm(SLOTS_ALL, IN[NC]), vm(15, 32, IN[NC]), vm(XN, 16, last), vm(3, 16, last),
        vm(ZN, XN, 2, 16, OUT[NC] // 2),
        vm(2, 16, 128), vm(7, 16, 128), vm(2, 16, 128), vm(15, 16, 128),
        vm(max(max(tiles) for tiles in SENT_ALL), 16, 128),
        pltpu.SemaphoreType.DMA((5,)),
        pltpu.SemaphoreType.DMA((4,)), pltpu.SemaphoreType.DMA((RECV_COUNT,)),
    ]
    arrays = (tokens.reshape(TOK, D), slot_weight, pattern, w_in, w_out.reshape(2 * FS, D))
    hbm = pl.BlockSpec(memory_space=pltpu.HBM)
    vmem = pl.BlockSpec(memory_space=pltpu.VMEM)
    mixed = pl.pallas_call(
        kernel,
        out_shape=pltpu.VMEM((TOK, D), BF16),
        in_specs=[hbm, hbm, hbm, hbm, hbm],
        out_specs=vmem,
        scratch_shapes=scratch,
        compiler_params=pltpu.CompilerParams(
            collective_id=0, has_side_effects=True, vmem_limit_bytes=40 << 20),
        name="layer",
    )(*(pltpu.with_memory_space_constraint(a, pltpu.HBM) for a in arrays))
    return mixed.reshape(tokens.shape)


def solution(mesh):
    in_specs = (
        P("clip", "seq", None),
        P(),
        P("seq", None),
        P("seq", None, "clip"),
        P("seq", "clip", None),
    )
    return jax.shard_map(
        local, mesh=mesh, in_specs=in_specs, out_specs=P("clip", "seq", None), check_vma=False)
```
